512 devices in a mesh: row: 32 (over z, x), col: 16 (over y, core).
Axes of the slice: x: 4, y: 8, z: 8, core: 2. Of those that a mesh axis runs over, the one named last changes fastest.
Arguments:
- trail_inverse: bfloat16 [12288, 12288], P('row', 'col'), may hold values from -6 to 6
- panels: bfloat16 [4, 12288, 512], P(None, 'row', 'col'), may hold values from -0.0625 to 0.0625
- couplings: bfloat16 [3, 512, 512], replicated, may hold values from -0.25 to 0.25
- diag_terms: float32 [4, 512, 512], P(None, None, 'col'), may hold values from -4 to 4
- listed: int32 [64], replicated, may hold values from 0 to 95, as said below
Outputs:
- panel_inverse: bfloat16 [4, 12288, 512], P(None, 'row', 'col')
- diag_inverse: float32 [4, 512, 512], P(None, None, 'col')
The draws below stay inside these ranges and needn't reach their ends.
Inputs may be any that keep to these rules, and one draw needn't show every extreme that they name: `listed`: 64 distinct trailing block numbers, including 0 and 95.
All inputs are finite; a program needn't handle non-finite values.
Results may differ from the reference program's by a relative error of at most 0.0049.
Values may be sent and summed in bfloat16 or wider, within the bound.
A program may use at most 64 MiB of HBM per device.

```python
import jax
import jax.numpy as jnp
from jax import lax

BS = 128
W = 512
SUPER = 4
NB = 96
NL = 64
TRAIL = 12288
N_COL = 16


def draw_listed(key, part):
    key = jax.random.fold_in(key, 7)
    inner = jax.random.permutation(key, NB - 2)[:NL - 2].astype(jnp.int32) + 1
    first = jnp.zeros((1,), jnp.int32)
    last = jnp.full((1,), NB - 1, jnp.int32)
    return jnp.concatenate([first, inner, last]).astype(jnp.int32)


def block_levels(rng, extent, cuts, low, high):
    def one(dim, shards_of):
        draws = jax.random.uniform(jax.random.fold_in(jax.random.fold_in(rng, 6), dim), (shards_of,), jnp.float32, low / len(cuts), high / len(cuts))
        return jnp.repeat(jnp.exp(draws), extent[dim] // shards_of).reshape((-1,) + (1,) * (len(extent) - dim - 1))

    factor_of = one(*cuts[0])
    for cut in cuts[1:]:
        factor_of = factor_of * one(*cut)
    return factor_of


def bell_draw(own_key, extent, width, reach, cuts=(), held_as=jnp.bfloat16):
    loudness = block_levels(own_key, extent, cuts, -0.22, 0.18) if cuts else 1.0
    values = jax.random.normal(own_key, extent, jnp.float32) * width * loudness
    return jnp.minimum(jnp.maximum(values, -reach), reach).astype(held_as)


def setup_inputs(seed: int = 0) -> dict:
    key_list = jax.random.split(jax.random.key(seed), 6)
    return {
        "trail_inverse": bell_draw(key_list[0], (TRAIL, TRAIL), 1.0, 6.0, ((0, 32), (1, 16))),
        "panels": bell_draw(key_list[1], (SUPER, TRAIL, W), (NL * BS) ** -0.5, 0.0625, ((1, 32), (2, 16))),
        "couplings": bell_draw(key_list[2], (SUPER - 1, W, W), W ** -0.5, 0.25),
        "diag_terms": bell_draw(key_list[3], (SUPER, W, W), 0.5, 4.0, ((2, 16),), jnp.float32),
        "listed": draw_listed(jax.random.fold_in(key_list[5], 71), 0),
    }


def reference(trail_inverse, panels, couplings, diag_terms, listed):
    blocks = jnp.arange(NB, dtype=jnp.int32)
    listed_hit = jnp.any(listed[:, None] == blocks[None, :], axis=0)
    row_mask = jnp.repeat(listed_hit.astype(jnp.float32), BS)[:, None]
    span = (NB * BS) // N_COL
    results = []
    diagonals = []
    prev_result = None
    prev_block = None
    for step in range(SUPER):
        masked = (panels[step].astype(jnp.float32) * row_mask).astype(jnp.bfloat16)
        summed = jnp.zeros((NB * BS, W), jnp.float32)
        for column in range(N_COL):
            partial_term = jnp.dot(trail_inverse[:, column * span:(column + 1) * span],
                                   masked[column * span:(column + 1) * span],
                                   preferred_element_type=jnp.float32)
            summed = summed + partial_term
        if step > 0:
            carried = jnp.dot(prev_result, couplings[step - 1], preferred_element_type=jnp.float32)
            summed = summed + carried
        result = (-(summed * row_mask)).astype(jnp.bfloat16)
        block = diag_terms[step] - jnp.dot(masked.T, result, preferred_element_type=jnp.float32)
        if step > 0:
            coupling32 = couplings[step - 1].astype(jnp.float32)
            block = block + jnp.dot(carried.T, masked.astype(jnp.float32), precision=lax.Precision.HIGHEST)
            inner = jnp.dot(prev_block, coupling32, precision=lax.Precision.HIGHEST)
            block = block + jnp.dot(coupling32.T, inner, precision=lax.Precision.HIGHEST)
        results.append(result)
        diagonals.append(block)
        prev_result = result
        prev_block = block
    return jnp.stack(results), jnp.stack(diagonals)
```

```python
import functools

import jax
import jax.numpy as jnp
from jax import lax
from jax.experimental import pallas as pl
from jax.experimental.pallas import tpu as pltpu
from jax.sharding import PartitionSpec as P

SUPER = 4
NX = 4
ROWS = 384
PIECE = 128
LAG = 2
MESH = pl.DeviceIdType.MESH
F32 = jnp.float32
BF16 = jnp.bfloat16
NT_DIMS = (((1,), (1,)), ((), ()))
TN_DIMS = (((0,), (0,)), ((), ()))


def iota(shape, dim):
    return lax.broadcasted_iota(jnp.int32, shape, dim)


def mod(value, size):
    return lax.rem(value + 2 * size, size)


def swap_halves(value):
    return pltpu.roll(value, 64, 1)


def kernel(
    ny,
    panels_ref, listed_ref, trail_ref, coup_ref, diag_ref,
    outp_ref, outd_ref,
    tp, cc, ct, vst, dgo, dgs, dgw, mw, ms, sp, rb, ss, zs, zb, zo, ps, pb, ev, eb1, eb2, fb,
    sem, zrecv, xrecv,
):
    nz = ny
    width = 64 * ny
    chain_rows = ROWS // ny
    tiles = width // 128
    row, col = lax.axis_index("row"), lax.axis_index("col")
    z, x = lax.div(row, NX), lax.rem(row, NX)
    y, h = lax.div(col, 2), lax.rem(col, 2)
    sibling = 1 - h

    def dev(xx, yy, zz, hh):
        return (zz * NX + xx, yy * 2 + hh)

    def remote(src, dst, send, recv, device):
        return pltpu.make_async_remote_copy(
            src_ref=src, dst_ref=dst, send_sem=send, recv_sem=recv,
            device_id=device, device_id_type=MESH,
        )

    def wait_bytes(ref, semaphore):
        pltpu.make_async_copy(ref, ref, semaphore).wait()

    (s_t, r_t, s_z, s_x, s_mw, r_mw, s_tp, r_tp, s_rs, r_rs, s_ss, r_ss, s_zb, r_zb,
     s_mf, r_mf, s_zo, r_zo, s_p, r_p, s_e, r_e1, r_e2, s_f, r_f, s_dg, r_dg,
     l_tp, l_cc, l_dg) = [sem.at[i] for i in range(30)]

    barrier = pltpu.get_barrier_semaphore()

    def greet(device):
        pl.semaphore_signal(barrier, inc=1, device_id=device, device_id_type=MESH)

    @pl.loop(1, 2 * ny)
    def _(step):
        greet((row, mod(col + step, 2 * ny)))

    @pl.loop(1, NX * nz)
    def _(step):
        greet((mod(row + step, NX * nz), col))

    @pl.when(y != z)
    def _():
        greet(dev(x, z, y, h))

    @pl.loop(0, nz)
    def _(zz):
        me = jnp.logical_and(jnp.logical_and(z == y, zz == z), h == 1)

        @pl.when(jnp.logical_not(me))
        def _():
            greet(dev(x, z, zz, 1))

    own_tp = pltpu.make_async_copy(trail_ref, tp.at[h], l_tp)
    own_tp.start()
    own_cc = pltpu.make_async_copy(coup_ref, cc, l_cc)
    own_cc.start()
    own_dg = pltpu.make_async_copy(diag_ref.at[x, pl.ds(64 * z, 64)], dgo, l_dg)
    own_dg.start()

    listed = listed_ref[...]

    def flag(block):
        return jnp.max(jnp.where(listed == block, 1.0, 0.0), axis=1, keepdims=True)

    lane = iota((1, ROWS), 1)
    piece_mask = jnp.where(
        lane < 128, flag(3 * row), jnp.where(lane < 256, flag(3 * row + 1), flag(3 * row + 2))
    )
    eye = jnp.where(iota((32, 32), 0) == iota((32, 32), 1), 1.0, 0.0).astype(BF16)
    for k in range(SUPER):
        turned = lax.dot_general(eye, panels_ref[k], NT_DIMS, preferred_element_type=F32)
        mw[h, y, 32 * k:32 * (k + 1), :] = (turned * piece_mask).astype(BF16)

    off_diagonal = jnp.where(y != z, 1, 0)
    pl.semaphore_wait(
        barrier,
        (2 * ny - 1) + (NX * nz - 1) + off_diagonal + h * (2 * ny - 1 + off_diagonal),
    )

    mine = mw.at[h, y]

    @pl.when(y != z)
    def _():
        remote(mine, ms.at[y * NX + x], s_t, r_t, dev(x, z, y, h)).start()

    @pl.when(y == z)
    def _():
        pltpu.make_async_copy(mine, ms.at[y * NX + x], r_t).start()

    send_tp = remote(trail_ref, tp.at[h], s_tp, r_tp, dev(x, y, z, sibling))
    send_tp.start()
    send_dg = remote(
        diag_ref.at[x, pl.ds(64 * z, 64)], dgs, s_dg, r_dg, dev(x, y, z, sibling)
    )
    send_dg.start()

    def near(step):
        half = lax.div(step + 1, 2)
        return jnp.where(lax.rem(step, 2) == 1, half, mod(-half, nz))

    home = ms.at[z * NX + x]
    wait_bytes(home, r_t)

    @pl.loop(1, nz)
    def _(step):
        delta = near(step)
        remote(home, home, s_z, zrecv.at[delta], dev(x, y, mod(z + delta, nz), h)).start()

    @pl.loop(1, ny)
    def _(step):
        remote(mine, mine, s_mw, r_mw, dev(x, mod(y + near(step), ny), z, h)).start()

    own_tp.wait()
    wait_bytes(tp.at[0], r_tp)

    @pl.loop(0, nz + LAG)
    def _(step):
        @pl.when(step < nz)
        def _():
            delta = near(step)
            slot = ms.at[mod(z - delta, nz) * NX + x]

            @pl.when(step > 0)
            def _():
                wait_bytes(slot, zrecv.at[delta])

            for dx in (1, 3, 2):
                remote(
                    slot, slot, s_x, xrecv.at[delta], dev(mod(x + dx, NX), y, z, h)
                ).start()

        @pl.when(step >= LAG)
        def _():
            delta = near(step - LAG)
            chunk = mod(z - delta, nz)
            wait_bytes(ms.at[pl.ds(0, NX - 1)], xrecv.at[delta])
            total = None
            for xx in range(NX):
                term = lax.dot_general(
                    tp[xx // 2, :, ROWS * (xx % 2):ROWS * (xx % 2 + 1)],
                    ms[chunk * NX + xx], NT_DIMS, preferred_element_type=F32,
                )
                total = term if total is None else total + term
            total = total.astype(BF16)
            lanes = pl.ds(pl.multiple_of(chunk * PIECE, PIECE), PIECE)
            for yy in range(ny):
                sp[yy, :, lanes] = total[chain_rows * yy:chain_rows * (yy + 1)]

            @pl.loop(1, ny)
            def _(i):
                to = mod(y + i, ny)
                remote(
                    sp.at[to, :, lanes], rb.at[i - 1, :, lanes], s_rs, r_rs, dev(x, to, z, h)
                ).start()

    own_cc.wait()
    wide_eye = jnp.where(iota((width, width), 0) == iota((width, width), 1), 1.0, 0.0)
    wide_eye = wide_eye.astype(BF16)
    group = lax.div(iota((width, 128), 1), 32)
    picks = iota((width, 128), 0) == col * 32 + lax.rem(iota((width, 128), 1), 32)
    for j in range(SUPER - 1):
        ct[j] = lax.dot_general(
            wide_eye, cc[j], NT_DIMS, preferred_element_type=F32
        ).astype(BF16)
    above = None
    for j in reversed(range(SUPER)):
        chosen = jnp.where(jnp.logical_and(picks, group == j), 1.0, 0.0)
        if above is not None:
            chosen = chosen + jnp.dot(cc[j], above, preferred_element_type=F32)
        above = chosen.astype(BF16)
        vst[j] = above

    own_dg.wait()
    wait_bytes(dgs, r_dg)
    dgw[...] = jnp.zeros_like(dgw)
    dgw[0, :, 0:32] = dgo[...]
    dgw[1, :, 0:32] = dgs[...]
    both = dgw[0] + pltpu.roll(dgw[1], 32, 1)
    diag_packed = both[0:32] + swap_halves(both[32:64])

    wait_bytes(mw.at[0, pl.ds(0, ny - 1)], r_mw)
    send_mf = remote(mw.at[h], mw.at[h], s_mf, r_mf, dev(x, y, z, sibling))
    send_mf.start()

    wait_bytes(rb, r_rs)
    for t in range(ny):
        part = slice(128 * t, 128 * (t + 1))
        total = sp[y, :, part].astype(F32)
        for i in range(ny - 1):
            total = total + rb[i, :, part].astype(F32)
        ss[h, :, part] = total
    send_ss = remote(ss.at[h], ss.at[h], s_ss, r_ss, dev(x, y, z, sibling))
    send_ss.start()
    wait_bytes(ss.at[0], r_ss)

    block = lax.shift_right_logical(
        ROWS * row + chain_rows * y + iota((chain_rows, 1), 0), 7
    )
    row_mask = jnp.max(jnp.where(listed == block, 1.0, 0.0), axis=1, keepdims=True)
    quarter = lax.div(iota((chain_rows, 128), 1), 32)
    low = iota((chain_rows, 128), 1) < 64
    result = None
    kept = []
    for k in range(SUPER):
        found = []
        for t in range(tiles):
            tile = None
            for g in range(4):
                yy = 2 * t + g // 2
                source = ss[g % 2, :, 128 * yy:128 * (yy + 1)]
                shift = (32 * (g - k)) % 128
                if shift:
                    source = pltpu.roll(source, shift, 1)
                tile = source if tile is None else jnp.where(quarter == g, source, tile)
            found.append(tile)
        summed = jnp.concatenate(found, axis=1) if tiles > 1 else found[0]
        carried = jnp.zeros_like(summed)
        if k > 0:
            carried = jnp.dot(result, cc[k - 1], preferred_element_type=F32)
            summed = summed + carried
        result = (-(summed * row_mask)).astype(BF16)
        kept.append(jnp.where(h == 0, result.astype(F32), carried))
    for pair in range(SUPER // 2):
        for t in range(tiles):
            part = slice(128 * t, 128 * (t + 1))
            first, second = kept[2 * pair][:, part], kept[2 * pair + 1][:, part]
            lanes = slice(128 * pair, 128 * (pair + 1))
            zs[2 * t, :, lanes] = jnp.where(low, first, swap_halves(second)).astype(BF16)
            zs[2 * t + 1, :, lanes] = jnp.where(low, swap_halves(first), second).astype(BF16)

    own_rows = pl.ds(pl.multiple_of(chain_rows * y, 16), chain_rows)

    @pl.loop(1, ny)
    def _(i):
        to = mod(y + i, ny)
        remote(zs.at[to], zb.at[own_rows], s_zb, r_zb, dev(x, to, z, h)).start()

    zb[own_rows, :] = zs[y]
    wait_bytes(mw.at[0], r_mf)
    wait_bytes(zb.at[pl.ds(0, chain_rows * (ny - 1))], r_zb)

    @pl.when(h == 0)
    def _():
        remote(zb, zo, s_zo, r_zo, dev(x, y, z, 1)).start()

    low32 = iota((32, 128), 1) < 64
    for k in range(SUPER):
        left = jnp.concatenate(
            [mw[c % 2, c // 2, 32 * k:32 * (k + 1), :] for c in range(2 * ny)], axis=0
        )
        pair = k // 2
        product = jnp.dot(
            left, zb[:, 128 * pair:128 * (pair + 1)], preferred_element_type=F32
        )
        for zz in range(nz):
            upper = product[64 * zz:64 * zz + 32]
            lower = product[64 * zz + 32:64 * zz + 64]
            if k % 2 == 0:
                packed = jnp.where(low32, upper, swap_halves(lower))
            else:
                packed = jnp.where(low32, swap_halves(upper), lower)
            ps[k * nz + zz] = packed.astype(BF16)

    @pl.loop(1, NX * nz)
    def _(i):
        xx = mod(x + lax.div(i, nz), NX)
        zz = mod(z + lax.rem(i, nz), nz)
        remote(ps.at[xx * nz + zz], pb.at[i - 1], s_p, r_p, dev(xx, y, zz, h)).start()

    @pl.when(h == 0)
    def _():
        for k in range(SUPER):
            tile = zb[:, 128 * (k // 2):128 * (k // 2 + 1)].astype(F32)
            tile = swap_halves(tile) if k % 2 else tile
            outp_ref[k] = tile[:, 0:32].astype(BF16)

    @pl.when(h == 1)
    def _():
        wait_bytes(zo, r_zo)
        for k in range(SUPER):
            tile = zo[:, 128 * (k // 2):128 * (k // 2 + 1)].astype(F32)
            tile = pltpu.roll(tile, 32 if k % 2 else 96, 1)
            outp_ref[k] = tile[:, 0:32].astype(BF16)

    wait_bytes(pb, r_p)
    total = ps[x * nz + z].astype(F32)
    for i in range(NX * nz - 1):
        total = total + pb[i].astype(F32)
    ev[...] = jnp.where(h == 0, diag_packed - total, total).astype(BF16)

    @pl.loop(0, 2 * ny)
    def _(i):
        yy, hh = lax.div(i, 2), lax.rem(i, 2)

        @pl.when(h == 0)
        def _():
            @pl.when(i == col)
            def _():
                pltpu.make_async_copy(ev, eb1.at[y], r_e1).start()

            @pl.when(i != col)
            def _():
                remote(ev, eb1.at[y], s_e, r_e1, dev(x, yy, z, hh)).start()

        @pl.when(h == 1)
        def _():
            me = jnp.logical_and(i == col, y == z)

            @pl.when(me)
            def _():
                pltpu.make_async_copy(ev, eb2.at[z], r_e2).start()

            @pl.when(jnp.logical_not(me))
            def _():
                remote(ev, eb2.at[z], s_e, r_e2, dev(x, yy, y, hh)).start()

    wait_bytes(eb1, r_e1)
    wait_bytes(eb2, r_e2)
    upper, lower = [], []
    for t in range(tiles):
        first, second = eb1[2 * t].astype(F32), eb1[2 * t + 1].astype(F32)
        upper.append(jnp.where(low32, first, swap_halves(second)))
        lower.append(jnp.where(low32, swap_halves(first), second))
    if tiles > 1:
        upper = jnp.concatenate(upper, axis=1)
        lower = jnp.concatenate(lower, axis=1)
    else:
        upper, lower = upper[0], lower[0]
    straight = jnp.concatenate([upper, lower], axis=0).astype(BF16)
    stack = []
    for b in range(nz):
        value = eb2[b].astype(F32)
        stack += [value, swap_halves(value)]
    stack = jnp.concatenate(stack, axis=0).astype(BF16)
    right = vst[x]
    turned = lax.dot_general(stack, right, TN_DIMS, preferred_element_type=F32)
    own = jnp.dot(straight, right, preferred_element_type=F32) + turned[0:64]
    mine_f = fb.at[x * nz + z]
    mine_f[...] = own.astype(BF16)

    @pl.loop(1, NX * nz)
    def _(i):
        xx = mod(x + lax.div(i, nz), NX)
        zz = mod(z + lax.rem(i, nz), nz)
        remote(mine_f, mine_f, s_f, r_f, dev(xx, y, zz, h)).start()

    wait_bytes(fb.at[pl.ds(0, NX * nz - 1)], r_f)
    state = fb[pl.ds(0, nz)].reshape(width, 128).astype(F32)
    for j in range(SUPER - 1):
        high = state.astype(BF16)
        rest = (state - high.astype(F32)).astype(BF16)
        moved = jnp.dot(
            ct[j], jnp.concatenate([high, rest], axis=1), preferred_element_type=F32
        )
        moved = moved[:, 0:128] + moved[:, 128:256]
        added = fb[pl.ds((j + 1) * nz, nz)].reshape(width, 128).astype(F32)
        state = added + jnp.where(group > j, moved, state)
    for k in range(SUPER):
        outd_ref[k] = (pltpu.roll(state, 128 - 32 * k, 1) if k else state)[:, 0:32]

    @pl.when(y != z)
    def _():
        wait_bytes(home, s_t)

    wait_bytes(tp.at[0], s_tp)
    wait_bytes(dgs, s_dg)
    wait_bytes(ms.at[pl.ds(0, nz - 1)], s_z)
    wait_bytes(mw.at[0, pl.ds(0, ny - 1)], s_mw)
    wait_bytes(ms.at[pl.ds(0, (NX - 1) * nz)], s_x)
    wait_bytes(rb, s_rs)
    wait_bytes(mw.at[0], s_mf)
    wait_bytes(ss.at[0], s_ss)
    wait_bytes(zb.at[pl.ds(0, chain_rows * (ny - 1))], s_zb)

    @pl.when(h == 0)
    def _():
        wait_bytes(zo, s_zo)

    wait_bytes(pb, s_p)
    wait_bytes(eb1.at[pl.ds(0, ny - 1)], s_e)
    wait_bytes(eb2.at[pl.ds(0, ny - 1)], s_e)

    wait_bytes(ev, s_e)

    @pl.when(jnp.logical_and(h == 1, y != z))
    def _():
        wait_bytes(ev, s_e)

    wait_bytes(fb.at[pl.ds(0, NX * nz - 1)], s_f)


def on_device(trail_inverse, panels, couplings, diag_terms, listed):
    ny = lax.axis_size("col") // 2
    nz = ny
    width = 64 * ny
    chain_rows = ROWS // ny
    vmem = pl.BlockSpec(memory_space=pltpu.VMEM)
    anywhere = pl.BlockSpec(memory_space=pl.ANY)
    return pl.pallas_call(
        functools.partial(kernel, ny),
        out_shape=(
            jax.ShapeDtypeStruct((SUPER, ROWS, 32), BF16),
            jax.ShapeDtypeStruct((SUPER, width, 32), F32),
        ),
        in_specs=[vmem, vmem, anywhere, anywhere, anywhere],
        out_specs=(vmem, vmem),
        scratch_shapes=[
            pltpu.VMEM((2, ROWS, 768), BF16),
            pltpu.VMEM((SUPER - 1, width, width), BF16),
            pltpu.VMEM((SUPER - 1, width, width), BF16),
            pltpu.VMEM((SUPER, width, 128), BF16),
            pltpu.VMEM((64, 32), F32),
            pltpu.VMEM((64, 32), F32),
            pltpu.VMEM((2, 64, 128), F32),
            pltpu.VMEM((2, ny, PIECE, ROWS), BF16),
            pltpu.VMEM((nz * NX, PIECE, ROWS), BF16),
            pltpu.VMEM((ny, chain_rows, 128 * ny), BF16),
            pltpu.VMEM((ny - 1, chain_rows, 128 * ny), BF16),
            pltpu.VMEM((2, chain_rows, 128 * ny), F32),
            pltpu.VMEM((ny, chain_rows, 256), BF16),
            pltpu.VMEM((ROWS, 256), BF16),
            pltpu.VMEM((ROWS, 256), BF16),
            pltpu.VMEM((NX * nz, 32, 128), BF16),
            pltpu.VMEM((NX * nz - 1, 32, 128), BF16),
            pltpu.VMEM((32, 128), BF16),
            pltpu.VMEM((ny, 32, 128), BF16),
            pltpu.VMEM((nz, 32, 128), BF16),
            pltpu.VMEM((NX * nz, 64, 128), BF16),
            pltpu.SemaphoreType.DMA((30,)),
            pltpu.SemaphoreType.DMA((nz,)),
            pltpu.SemaphoreType.DMA((nz,)),
        ],
        compiler_params=pltpu.CompilerParams(
            collective_id=0, has_side_effects=True, vmem_limit_bytes=48 * 1024 * 1024
        ),
        name="chain",
    )(panels, listed.reshape(1, -1), trail_inverse, couplings, diag_terms)


def solution(mesh):
    in_specs = (P("row", "col"), P(None, "row", "col"), P(), P(None, None, "col"), P())
    out_specs = (P(None, "row", "col"), P(None, None, "col"))
    return jax.shard_map(
        on_device, mesh=mesh, in_specs=in_specs, out_specs=out_specs, check_vma=False
    )
```

```python
import functools

import jax
import jax.numpy as jnp
from jax import lax
from jax.experimental import pallas as pl
from jax.experimental.pallas import tpu as pltpu
from jax.sharding import PartitionSpec as P

SUPER = 4
NX = 4
ROWS = 384
PIECE = 128
LAG = 3
MESH = pl.DeviceIdType.MESH
F32 = jnp.float32
BF16 = jnp.bfloat16
NT_DIMS = (((1,), (1,)), ((), ()))
TN_DIMS = (((0,), (0,)), ((), ()))


def iota(shape, dim):
    return lax.broadcasted_iota(jnp.int32, shape, dim)


def mod(value, size):
    value = jnp.where(value < 0, value + size, value)
    return jnp.where(value >= size, value - size, value)


def swap_halves(value):
    return pltpu.roll(value, 64, 1)


def kernel(
    ny,
    panels_ref, listed_ref, trail_ref, coup_ref, diag_ref,
    outp_ref, outd_ref,
    tp, cc, ct, vst, dgo, dgs, mw, ms, sp, rb, ss, zs, zb, zo, ps, pb, ev, eb1, eb2, fb,
    sem, zrecv, xrecv, yrecv,
):
    nz = ny
    width = 64 * ny
    chain_rows = ROWS // ny
    tiles = width // 128
    row, col = lax.axis_index("row"), lax.axis_index("col")
    z, x = lax.div(row, NX), lax.rem(row, NX)
    y, h = lax.div(col, 2), lax.rem(col, 2)
    sibling = 1 - h

    def dev(xx, yy, zz, hh):
        return (zz * NX + xx, yy * 2 + hh)

    def remote(src, dst, send, recv, device):
        return pltpu.make_async_remote_copy(
            src_ref=src, dst_ref=dst, send_sem=send, recv_sem=recv,
            device_id=device, device_id_type=MESH,
        )

    def wait_bytes(ref, semaphore):
        pltpu.make_async_copy(ref, ref, semaphore).wait()

    (s_t, r_t, s_z, s_x, s_mw, r_x2, s_xh, s_tp, r_tp, s_rs, r_rs, s_ss, r_ss, s_zb, r_zb,
     s_mf, r_mf, s_zo, r_zo, s_p, r_p, s_e, r_e1, r_e2, s_f, r_f, s_dg, r_dg,
     l_tp, l_cc, l_dg) = [sem.at[i] for i in range(31)]

    barrier = pltpu.get_barrier_semaphore()

    def greet(device):
        pl.semaphore_signal(barrier, inc=1, device_id=device, device_id_type=MESH)

    greet(dev(x, y, z, sibling))
    for step in (1, nz - 1) if nz > 2 else (1,):
        greet(dev(x, y, mod(z + step, nz), h))
    for step in range(1, NX):
        greet(dev(mod(x + step, NX), y, z, h))
    for step in range(1, ny):
        greet(dev(x, mod(y + step, ny), z, h))

    @pl.when(y != z)
    def _():
        greet(dev(x, z, y, h))

    own_tp = pltpu.make_async_copy(trail_ref, tp.at[h], l_tp)
    own_tp.start()
    own_cc = pltpu.make_async_copy(coup_ref, cc, l_cc)
    own_cc.start()
    diag_tile = diag_ref.at[x, :, pl.ds(pl.multiple_of(lax.div(z, 2) * 128, 128), 128)]
    own_dg = pltpu.make_async_copy(diag_tile, dgo, l_dg)
    own_dg.start()

    listed = listed_ref[...]

    def flag(block):
        return jnp.max(jnp.where(listed == block, 1.0, 0.0), axis=1, keepdims=True)

    lane = iota((1, ROWS), 1)
    piece_mask = jnp.where(
        lane < 128, flag(3 * row), jnp.where(lane < 256, flag(3 * row + 1), flag(3 * row + 2))
    )
    for k in range(SUPER):
        turned = panels_ref[k].astype(F32)
        mw[h, y, 32 * k:32 * (k + 1), :] = (turned * piece_mask).astype(BF16)

    pl.semaphore_wait(
        barrier, min(2, nz - 1) + NX + ny - 1 + jnp.where(y != z, 1, 0)
    )

    mine = mw.at[h, y]

    @pl.when(y != z)
    def _():
        remote(mine, ms.at[y * NX + x], s_t, r_t, dev(x, z, y, h)).start()

    @pl.when(y == z)
    def _():
        pltpu.make_async_copy(mine, ms.at[y * NX + x], r_t).start()

    send_tp = remote(trail_ref, tp.at[h], s_tp, r_tp, dev(x, y, z, sibling))
    send_tp.start()
    send_dg = remote(diag_tile, dgs, s_dg, r_dg, dev(x, y, z, sibling))
    send_dg.start()

    def near(step):
        half = lax.div(step + 1, 2)
        return jnp.where(lax.rem(step, 2) == 1, half, mod(-half, nz))

    home = ms.at[z * NX + x]
    right, left = dev(mod(x + 1, NX), y, z, h), dev(mod(x - 1, NX), y, z, h)
    wait_bytes(home, r_t)

    own_tp.wait()
    wait_bytes(tp.at[0], r_tp)

    @pl.loop(0, nz + LAG)
    def _(step):
        @pl.when(step < nz)
        def _():
            delta = near(step)
            slot = ms.at[mod(z - delta, nz) * NX + x]
            wide = mw.at[h, mod(y - delta, ny)]
            ahead = lax.rem(step, 2) == 1
            z_next = mod(z + jnp.where(ahead, 1, -1), nz)
            y_next = mod(y + jnp.where(ahead, 1, -1), ny)

            @pl.when(step > 0)
            def _():
                wait_bytes(slot, zrecv.at[step])

            @pl.when(step == 0)
            def _():
                remote(slot, slot, s_z, zrecv.at[1], dev(x, y, mod(z + 1, nz), h)).start()

            @pl.when(step < nz - 2)
            def _():
                remote(slot, slot, s_z, zrecv.at[step + 2], dev(x, y, z_next, h)).start()

            remote(slot, slot, s_x, xrecv.at[0, step], right).start()
            remote(slot, slot, s_x, xrecv.at[1, step], left).start()

            @pl.when(step > 0)
            def _():
                wait_bytes(wide, yrecv.at[step])

            @pl.when(step == 0)
            def _():
                remote(wide, wide, s_mw, yrecv.at[1], dev(x, mod(y + 1, ny), z, h)).start()

            @pl.when(step < ny - 2)
            def _():
                remote(wide, wide, s_mw, yrecv.at[step + 2], dev(x, y_next, z, h)).start()

        @pl.when(jnp.logical_and(step >= 1, step <= nz))
        def _():
            at = step - 1
            first = mod(z - near(at), nz) * NX
            for way, source, to, rows in ((0, x - 1, right, 0), (1, x + 1, left, 64)):
                slot = ms.at[first + mod(source, NX)]
                wait_bytes(slot, xrecv.at[way, at])
                half = slot.at[pl.ds(rows, 64)]
                remote(half, half, s_xh, xrecv.at[2, at], to).start()

        @pl.when(step >= LAG)
        def _():
            at = step - LAG
            chunk = mod(z - near(at), nz)
            wait_bytes(home, xrecv.at[2, at])
            total = None
            for xx in range(NX):
                term = lax.dot_general(
                    tp[xx // 2, :, ROWS * (xx % 2):ROWS * (xx % 2 + 1)],
                    ms[chunk * NX + xx], NT_DIMS, preferred_element_type=F32,
                )
                total = term if total is None else total + term
            total = total.astype(BF16)
            lanes = pl.ds(pl.multiple_of(chunk * PIECE, PIECE), PIECE)
            for yy in range(ny):
                sp[yy, :, lanes] = total[chain_rows * yy:chain_rows * (yy + 1)]

            for i in range(1, ny):
                to = mod(y + i, ny)
                remote(
                    sp.at[to, :, lanes], rb.at[i - 1, :, lanes], s_rs, r_rs, dev(x, to, z, h)
                ).start()

    own_cc.wait()
    wide_eye = jnp.where(iota((width, width), 0) == iota((width, width), 1), 1.0, 0.0)
    wide_eye = wide_eye.astype(BF16)
    group = lax.div(iota((width, 128), 1), 32)
    picks = iota((width, 128), 0) == col * 32 + lax.rem(iota((width, 128), 1), 32)
    for j in range(SUPER - 1):
        ct[j] = lax.dot_general(
            wide_eye, cc[j], NT_DIMS, preferred_element_type=F32
        ).astype(BF16)
    above = None
    for j in reversed(range(SUPER)):
        chosen = jnp.where(jnp.logical_and(picks, group == j), 1.0, 0.0)
        if above is not None:
            chosen = chosen + jnp.dot(cc[j], above, preferred_element_type=F32)
        above = chosen.astype(BF16)
        vst[j] = above

    own_dg.wait()
    wait_bytes(dgs, r_dg)
    both = jnp.concatenate([dgo[...], dgs[...], jnp.zeros((64, 128), F32)], axis=0)
    both = jnp.where(lax.rem(z, 2) == 0, both, swap_halves(both)).T
    diag_packed = jnp.where(iota((32, 128), 1) < 64, both[0:32], swap_halves(both[32:64]))

    send_mf = remote(mw.at[h], mw.at[h], s_mf, r_mf, dev(x, y, z, sibling))
    send_mf.start()

    wait_bytes(rb, r_rs)
    for t in range(ny):
        part = slice(128 * t, 128 * (t + 1))
        total = sp[y, :, part].astype(F32)
        for i in range(ny - 1):
            total = total + rb[i, :, part].astype(F32)
        ss[h, :, part] = total
    send_ss = remote(ss.at[h], ss.at[h], s_ss, r_ss, dev(x, y, z, sibling))
    send_ss.start()
    wait_bytes(ss.at[0], r_ss)

    block = lax.shift_right_logical(
        ROWS * row + chain_rows * y + iota((chain_rows, 1), 0), 7
    )
    row_mask = jnp.max(jnp.where(listed == block, 1.0, 0.0), axis=1, keepdims=True)
    quarter = lax.div(iota((chain_rows, 128), 1), 32)
    low = iota((chain_rows, 128), 1) < 64
    result = None
    kept = []
    for k in range(SUPER):
        found = []
        for t in range(tiles):
            tile = None
            for g in range(4):
                yy = 2 * t + g // 2
                source = ss[g % 2, :, 128 * yy:128 * (yy + 1)]
                shift = (32 * (g - k)) % 128
                if shift:
                    source = pltpu.roll(source, shift, 1)
                tile = source if tile is None else jnp.where(quarter == g, source, tile)
            found.append(tile)
        summed = jnp.concatenate(found, axis=1) if tiles > 1 else found[0]
        carried = jnp.zeros_like(summed)
        if k > 0:
            carried = jnp.dot(result, cc[k - 1], preferred_element_type=F32)
            summed = summed + carried
        result = (-(summed * row_mask)).astype(BF16)
        kept.append(jnp.where(h == 0, result.astype(F32), carried))
    for pair in range(SUPER // 2):
        for t in range(tiles):
            part = slice(128 * t, 128 * (t + 1))
            first, second = kept[2 * pair][:, part], kept[2 * pair + 1][:, part]
            lanes = slice(128 * pair, 128 * (pair + 1))
            zs[2 * t, :, lanes] = jnp.where(low, first, swap_halves(second)).astype(BF16)
            zs[2 * t + 1, :, lanes] = jnp.where(low, swap_halves(first), second).astype(BF16)

    own_rows = pl.ds(pl.multiple_of(chain_rows * y, 16), chain_rows)

    for i in range(1, ny):
        to = mod(y + i, ny)
        remote(zs.at[to], zb.at[own_rows], s_zb, r_zb, dev(x, to, z, h)).start()

    zb[own_rows, :] = zs[y]
    wait_bytes(mw.at[0], r_mf)
    wait_bytes(zb.at[pl.ds(0, chain_rows * (ny - 1))], r_zb)

    @pl.when(h == 0)
    def _():
        remote(zb, zo, s_zo, r_zo, dev(x, y, z, 1)).start()

    low32 = iota((32, 128), 1) < 64
    for k in range(SUPER):
        left = jnp.concatenate(
            [mw[c % 2, c // 2, 32 * k:32 * (k + 1), :] for c in range(2 * ny)], axis=0
        )
        pair = k // 2
        product = jnp.dot(
            left, zb[:, 128 * pair:128 * (pair + 1)], preferred_element_type=F32
        )
        for zz in range(nz):
            upper = product[64 * zz:64 * zz + 32]
            lower = product[64 * zz + 32:64 * zz + 64]
            if k % 2 == 0:
                packed = jnp.where(low32, upper, swap_halves(lower))
            else:
                packed = jnp.where(low32, swap_halves(upper), lower)
            ps[k * nz + zz] = packed.astype(BF16)

    for i in range(1, NX * nz):
        xx, zz = mod(x + i // nz, NX), mod(z + i % nz, nz)
        remote(ps.at[xx * nz + zz], pb.at[i - 1], s_p, r_p, dev(xx, y, zz, h)).start()

    own_lane = 64 * lax.div(iota((128, 256), 0), 32) + 32 * h + lax.rem(iota((128, 256), 0), 32)
    own_lane = jnp.where(iota((128, 256), 1) == own_lane, 1.0, 0.0).astype(BF16)

    def write_panel(source):
        turned = lax.dot_general(own_lane, source[...], NT_DIMS, preferred_element_type=F32)
        outp_ref[...] = turned.astype(BF16).reshape(SUPER, 32, ROWS)

    @pl.when(h == 0)
    def _():
        write_panel(zb)

    @pl.when(h == 1)
    def _():
        wait_bytes(zo, r_zo)
        write_panel(zo)

    wait_bytes(pb, r_p)
    total = ps[x * nz + z].astype(F32)
    for i in range(NX * nz - 1):
        total = total + pb[i].astype(F32)
    ev[...] = jnp.where(h == 0, diag_packed - total, total).astype(BF16)

    @pl.when(h == 0)
    def _():
        pltpu.make_async_copy(ev, eb1.at[y], r_e1).start()
        for i in range(1, 2 * ny):
            yy = mod(y + i // 2, ny)
            remote(ev, eb1.at[y], s_e, r_e1, dev(x, yy, z, i % 2)).start()

    @pl.when(h == 1)
    def _():
        for i in range(2 * ny):
            yy = mod(y + i // 2, ny)
            if i == 1:
                @pl.when(y == z)
                def _():
                    pltpu.make_async_copy(ev, eb2.at[z], r_e2).start()

                @pl.when(y != z)
                def _():
                    remote(ev, eb2.at[z], s_e, r_e2, dev(x, yy, y, 1)).start()
            else:
                remote(ev, eb2.at[z], s_e, r_e2, dev(x, yy, y, i % 2)).start()

    wait_bytes(eb1, r_e1)
    wait_bytes(eb2, r_e2)
    upper, lower = [], []
    for t in range(tiles):
        first, second = eb1[2 * t].astype(F32), eb1[2 * t + 1].astype(F32)
        upper.append(jnp.where(low32, first, swap_halves(second)))
        lower.append(jnp.where(low32, swap_halves(first), second))
    if tiles > 1:
        upper = jnp.concatenate(upper, axis=1)
        lower = jnp.concatenate(lower, axis=1)
    else:
        upper, lower = upper[0], lower[0]
    straight = jnp.concatenate([upper, lower], axis=0).astype(BF16)
    stack = []
    for b in range(nz):
        value = eb2[b].astype(F32)
        stack += [value, swap_halves(value)]
    stack = jnp.concatenate(stack, axis=0).astype(BF16)
    right = vst[x]
    turned = lax.dot_general(stack, right, TN_DIMS, preferred_element_type=F32)
    own = jnp.dot(straight, right, preferred_element_type=F32) + turned[0:64]
    mine_f = fb.at[x * nz + z]
    mine_f[...] = own.astype(BF16)
    for i in range(1, nz):
        remote(mine_f, mine_f, s_f, r_f, dev(x, y, mod(z + i, nz), h)).start()
    wait_bytes(fb.at[pl.ds(0, nz - 1)], r_f)
    mine_x = fb.at[pl.ds(pl.multiple_of(x * nz, nz), nz)]
    for i in (1, 3, 2):
        remote(mine_x, mine_x, s_f, r_x2, dev(mod(x + i, NX), y, z, h)).start()
    wait_bytes(fb.at[pl.ds(0, (NX - 1) * nz)], r_x2)
    state = fb[pl.ds(0, nz)].reshape(width, 128).astype(F32)
    for j in range(SUPER - 1):
        high = state.astype(BF16)
        rest = (state - high.astype(F32)).astype(BF16)
        moved = jnp.dot(
            ct[j], jnp.concatenate([high, rest], axis=1), preferred_element_type=F32
        )
        moved = moved[:, 0:128] + moved[:, 128:256]
        added = fb[pl.ds((j + 1) * nz, nz)].reshape(width, 128).astype(F32)
        state = added + jnp.where(group > j, moved, state)
    outd_ref[...] = state.T.reshape(SUPER, 32, width)

    @pl.when(y != z)
    def _():
        wait_bytes(home, s_t)

    wait_bytes(tp.at[0], s_tp)
    wait_bytes(dgs, s_dg)
    wait_bytes(ms.at[pl.ds(0, nz - 1)], s_z)
    wait_bytes(mw.at[0, pl.ds(0, ny - 1)], s_mw)
    wait_bytes(ms.at[pl.ds(0, 2 * nz)], s_x)
    wait_bytes(ms.at[pl.ds(0, nz)], s_xh)
    wait_bytes(rb, s_rs)
    wait_bytes(mw.at[0], s_mf)
    wait_bytes(ss.at[0], s_ss)
    wait_bytes(zb.at[pl.ds(0, chain_rows * (ny - 1))], s_zb)

    @pl.when(h == 0)
    def _():
        wait_bytes(zo, s_zo)

    wait_bytes(pb, s_p)
    wait_bytes(eb1.at[pl.ds(0, ny - 1)], s_e)
    wait_bytes(eb2.at[pl.ds(0, ny - 1)], s_e)

    wait_bytes(ev, s_e)

    @pl.when(jnp.logical_and(h == 1, y != z))
    def _():
        wait_bytes(ev, s_e)

    wait_bytes(fb.at[pl.ds(0, nz - 1)], s_f)
    wait_bytes(fb.at[pl.ds(0, (NX - 1) * nz)], s_f)


def on_device(trail_inverse, panels, couplings, diag_terms, listed):
    ny = lax.axis_size("col") // 2
    nz = ny
    width = 64 * ny
    chain_rows = ROWS // ny
    vmem = pl.BlockSpec(memory_space=pltpu.VMEM)
    anywhere = pl.BlockSpec(memory_space=pl.ANY)
    panel, diag = pl.pallas_call(
        functools.partial(kernel, ny),
        out_shape=(
            jax.ShapeDtypeStruct((SUPER, 32, ROWS), BF16),
            jax.ShapeDtypeStruct((SUPER, 32, width), F32),
        ),
        in_specs=[vmem, vmem, anywhere, anywhere, anywhere],
        out_specs=(vmem, vmem),
        scratch_shapes=[
            pltpu.VMEM((2, ROWS, 768), BF16),
            pltpu.VMEM((SUPER - 1, width, width), BF16),
            pltpu.VMEM((SUPER - 1, width, width), BF16),
            pltpu.VMEM((SUPER, width, 128), BF16),
            pltpu.VMEM((32, 128), F32),
            pltpu.VMEM((32, 128), F32),
            pltpu.VMEM((2, ny, PIECE, ROWS), BF16),
            pltpu.VMEM((nz * NX, PIECE, ROWS), BF16),
            pltpu.VMEM((ny, chain_rows, 128 * ny), BF16),
            pltpu.VMEM((ny - 1, chain_rows, 128 * ny), BF16),
            pltpu.VMEM((2, chain_rows, 128 * ny), F32),
            pltpu.VMEM((ny, chain_rows, 256), BF16),
            pltpu.VMEM((ROWS, 256), BF16),
            pltpu.VMEM((ROWS, 256), BF16),
            pltpu.VMEM((NX * nz, 32, 128), BF16),
            pltpu.VMEM((NX * nz - 1, 32, 128), BF16),
            pltpu.VMEM((32, 128), BF16),
            pltpu.VMEM((ny, 32, 128), BF16),
            pltpu.VMEM((nz, 32, 128), BF16),
            pltpu.VMEM((NX * nz, 64, 128), BF16),
            pltpu.SemaphoreType.DMA((31,)),
            pltpu.SemaphoreType.DMA((nz,)),
            pltpu.SemaphoreType.DMA((3, nz)),
            pltpu.SemaphoreType.DMA((ny,)),
        ],
        compiler_params=pltpu.CompilerParams(
            collective_id=0, has_side_effects=True, vmem_limit_bytes=60 * 1024 * 1024
        ),
        name="chain",
    )(
        panels.swapaxes(1, 2), listed.reshape(1, -1), trail_inverse, couplings,
        diag_terms.swapaxes(1, 2),
    )
    return panel.swapaxes(1, 2), diag.swapaxes(1, 2)


def solution(mesh):
    in_specs = (P("row", "col"), P(None, "row", "col"), P(), P(None, None, "col"), P())
    out_specs = (P(None, "row", "col"), P(None, None, "col"))
    return jax.shard_map(
        on_device, mesh=mesh, in_specs=in_specs, out_specs=out_specs, check_vma=False
    )
```

```python
import functools

import jax
import jax.numpy as jnp
from jax import lax
from jax.experimental import pallas as pl
from jax.experimental.pallas import tpu as pltpu
from jax.sharding import PartitionSpec as P

SUPER = 4
NX = 4
ROWS = 384
PIECE = 128
LAG = 3
ADD = 5
MESH = pl.DeviceIdType.MESH
F32 = jnp.float32
BF16 = jnp.bfloat16
NT_DIMS = (((1,), (1,)), ((), ()))
TN_DIMS = (((0,), (0,)), ((), ()))


def iota(shape, dim):
    return lax.broadcasted_iota(jnp.int32, shape, dim)


def mod(value, size):
    value = jnp.where(value < 0, value + size, value)
    return jnp.where(value >= size, value - size, value)


def split(value):
    high = value.astype(BF16)
    return [high, (value - high.astype(F32)).astype(BF16)]


def swap_halves(value):
    return pltpu.roll(value, 64, 1)


def kernel(
    ny,
    panels_ref, listed_ref, trail_ref, coup_ref, diag_ref,
    outp_ref, outd_ref,
    tp, cc, ct, vst, dgo, dgs, mw, ms, part, out, got, sp, rb, ss, zs, zb, zo, ps, pb, ev, eb1, eb2, fb,
    sem, zrecv, xrecv, precv, yrecv, frecv,
):
    nz = ny
    width = 64 * ny
    chain_rows = ROWS // ny
    tiles = width // 128
    row, col = lax.axis_index("row"), lax.axis_index("col")
    z, x = lax.div(row, NX), lax.rem(row, NX)
    y, h = lax.div(col, 2), lax.rem(col, 2)
    sibling = 1 - h

    def dev(xx, yy, zz, hh):
        return (zz * NX + xx, yy * 2 + hh)

    def remote(src, dst, send, recv, device):
        return pltpu.make_async_remote_copy(
            src_ref=src, dst_ref=dst, send_sem=send, recv_sem=recv,
            device_id=device, device_id_type=MESH,
        )

    def wait_bytes(ref, semaphore):
        pltpu.make_async_copy(ref, ref, semaphore).wait()

    (s_t, r_t, s_z, s_x, s_mw, s_p2, r_t2, s_eb, s_td, r_td, s_tp, r_tp, s_rs, r_rs, s_ss, r_ss, s_zb, r_zb,
     s_mf, r_mf, s_zo, r_zo, s_p, r_p, s_e, r_e1, r_e2, s_f, r_f, s_dg, r_dg,
     l_tp, l_cc, l_dg) = [sem.at[i] for i in range(34)]

    barrier = pltpu.get_barrier_semaphore()

    def greet(device):
        pl.semaphore_signal(barrier, inc=1, device_id=device, device_id_type=MESH)

    greet(dev(x, y, z, sibling))
    for step in (1, nz - 1) if nz > 2 else (1,):
        greet(dev(x, y, mod(z + step, nz), h))
    for step in range(1, NX):
        greet(dev(mod(x + step, NX), y, z, h))
    for step in range(1, ny):
        greet(dev(x, mod(y + step, ny), z, h))

    @pl.when(y != z)
    def _():
        greet(dev(x, z, y, h))

    pair = x + 1 - 2 * lax.rem(x, 2)
    inner = jnp.where(jnp.logical_or(x == 1, x == 2), 1, 0)

    def side_of(core):
        return jnp.where(core == inner, 0, 1)

    kept_side, given_side = side_of(h), 1 - side_of(h)
    own_tp = pltpu.make_async_copy(
        trail_ref.at[:, pl.ds(pl.multiple_of(kept_side * ROWS, ROWS), ROWS)], tp.at[h, 0], l_tp
    )
    own_tp.start()
    own_cc = pltpu.make_async_copy(coup_ref, cc, l_cc)
    own_cc.start()
    diag_tile = diag_ref.at[x, :, pl.ds(pl.multiple_of(lax.div(z, 2) * 128, 128), 128)]
    own_dg = pltpu.make_async_copy(diag_tile, dgo, l_dg)
    own_dg.start()

    listed = listed_ref[...]

    def flag(block):
        return jnp.max(jnp.where(listed == block, 1.0, 0.0), axis=1, keepdims=True)

    lane = iota((1, ROWS), 1)
    piece_mask = jnp.where(
        lane < 128, flag(3 * row), jnp.where(lane < 256, flag(3 * row + 1), flag(3 * row + 2))
    )
    for k in range(SUPER):
        turned = panels_ref[k].astype(F32)
        mw[h, y, 32 * k:32 * (k + 1), :] = (turned * piece_mask).astype(BF16)

    pl.semaphore_wait(
        barrier, min(2, nz - 1) + NX + ny - 1 + jnp.where(y != z, 1, 0)
    )

    mine = mw.at[h, y]
    landed = (r_t, r_t2)
    halves = [pl.ds(64 * half, 64) for half in range(2)]

    for half in range(2):
        target = ms.at[y * NX + x, halves[half]]

        @pl.when(y != z)
        def _():
            remote(mine.at[halves[half]], target, s_t, landed[half], dev(x, z, y, h)).start()

        @pl.when(y == z)
        def _():
            pltpu.make_async_copy(mine.at[halves[half]], target, landed[half]).start()

    given = trail_ref.at[:, pl.ds(pl.multiple_of(given_side * ROWS, ROWS), ROWS)]
    remote(given, tp.at[h, 1], s_tp, r_tp, dev(pair, y, z, h)).start()
    send_dg = remote(diag_tile, dgs, s_dg, r_dg, dev(x, y, z, sibling))
    send_dg.start()

    def near(step):
        half = lax.div(step + 1, 2)
        return jnp.where(lax.rem(step, 2) == 1, half, mod(-half, nz))

    home = ms.at[z * NX + x]
    own_cc.wait()
    wide_eye = jnp.where(iota((width, width), 0) == iota((width, width), 1), 1.0, 0.0)
    wide_eye = wide_eye.astype(BF16)
    group = lax.div(iota((width, 128), 1), 32)
    picks = iota((width, 128), 0) == col * 32 + lax.rem(iota((width, 128), 1), 32)
    for j in range(SUPER - 1):
        ct[j] = lax.dot_general(
            wide_eye, cc[j], NT_DIMS, preferred_element_type=F32
        ).astype(BF16)
    above = None
    for j in reversed(range(SUPER)):
        chosen = jnp.where(jnp.logical_and(picks, group == j), 1.0, 0.0)
        if above is not None:
            chosen = chosen + jnp.dot(cc[j], above, preferred_element_type=F32)
        above = chosen.astype(BF16)
        vst[j] = above

    own_dg.wait()
    wait_bytes(dgs, r_dg)
    both = jnp.concatenate([dgo[...], dgs[...], jnp.zeros((64, 128), F32)], axis=0)
    both = jnp.where(lax.rem(z, 2) == 0, both, swap_halves(both)).T
    diag_packed = jnp.where(iota((32, 128), 1) < 64, both[0:32], swap_halves(both[32:64]))

    own_tp.wait()
    wait_bytes(tp.at[0, 0], r_tp)
    remote(tp.at[h], tp.at[h], s_td, r_td, dev(x, y, z, sibling)).start()
    wait_bytes(tp.at[0], r_td)

    def relay_piece(step, half):
        slot = ms.at[mod(z - near(step), nz) * NX + x, halves[half]]
        z_next = mod(z + jnp.where(lax.rem(step, 2) == 1, 1, -1), nz)

        @pl.when(step > 0)
        def _():
            wait_bytes(slot, zrecv.at[half, step])

        @pl.when(step == 0)
        def _():
            wait_bytes(slot, landed[half])
            remote(slot, slot, s_z, zrecv.at[half, 1], dev(x, y, mod(z + 1, nz), h)).start()

        @pl.when(step < nz - 2)
        def _():
            remote(slot, slot, s_z, zrecv.at[half, step + 2], dev(x, y, z_next, h)).start()

        remote(slot, slot, s_x, xrecv.at[half, step], dev(3 - x, y, z, h)).start()

    def relay_wide(step):
        wide = mw.at[h, mod(y - near(step), ny)]
        y_next = mod(y + jnp.where(lax.rem(step, 2) == 1, 1, -1), ny)

        @pl.when(step > 0)
        def _():
            wait_bytes(wide, yrecv.at[step])

        @pl.when(step == 0)
        def _():
            remote(wide, wide, s_mw, yrecv.at[1], dev(x, mod(y + 1, ny), z, h)).start()

        @pl.when(step < ny - 2)
        def _():
            remote(wide, wide, s_mw, yrecv.at[step + 2], dev(x, y_next, z, h)).start()

    @pl.loop(0, nz + ADD)
    def _(step):
        @pl.when(step < nz)
        def _():
            relay_piece(step, 0)

        @pl.when(jnp.logical_and(step >= 1, step <= nz))
        def _():
            relay_piece(step - 1, 1)

        @pl.when(step < nz)
        def _():
            relay_wide(step)

        @pl.when(jnp.logical_and(step >= LAG, step < nz + LAG))
        def _():
            at = step - LAG
            chunk = mod(z - near(at), nz)
            for half in range(2):
                wait_bytes(home.at[halves[half]], xrecv.at[half, at])
            sums = [None, None]
            for core in range(2):
                piece = ms[chunk * NX + 2 * core + side_of(core)]
                for rows in range(2):
                    term = lax.dot_general(
                        tp[core, rows], piece, NT_DIMS, preferred_element_type=F32
                    )
                    sums[rows] = term if core == 0 else sums[rows] + term
            part[chunk] = sums[0]
            out[chunk] = sums[1].astype(BF16)
            remote(out.at[chunk], got.at[chunk], s_p2, precv.at[at], dev(pair, y, z, h)).start()

        @pl.when(step >= ADD)
        def _():
            at = step - ADD
            chunk = mod(z - near(at), nz)
            wait_bytes(got.at[chunk], precv.at[at])
            total = part[chunk] + got[chunk].astype(F32)
            total = total.astype(BF16)
            lanes = pl.ds(pl.multiple_of(chunk * PIECE, PIECE), PIECE)
            for yy in range(ny):
                sp[yy, :, lanes] = total[chain_rows * yy:chain_rows * (yy + 1)]

            for i in range(1, ny):
                to = mod(y + i, ny)
                remote(
                    sp.at[to, :, lanes], rb.at[i - 1, :, lanes], s_rs, r_rs, dev(x, to, z, h)
                ).start()

    send_mf = remote(mw.at[h], mw.at[h], s_mf, r_mf, dev(x, y, z, sibling))
    send_mf.start()

    wait_bytes(rb, r_rs)
    for t in range(ny):
        lanes = slice(128 * t, 128 * (t + 1))
        total = sp[y, :, lanes].astype(F32)
        for i in range(ny - 1):
            total = total + rb[i, :, lanes].astype(F32)
        ss[h, :, lanes] = total
    send_ss = remote(ss.at[h], ss.at[h], s_ss, r_ss, dev(x, y, z, sibling))
    send_ss.start()
    wait_bytes(ss.at[0], r_ss)

    block = lax.shift_right_logical(
        ROWS * row + chain_rows * y + iota((chain_rows, 1), 0), 7
    )
    row_mask = jnp.max(jnp.where(listed == block, 1.0, 0.0), axis=1, keepdims=True)
    quarter = lax.div(iota((chain_rows, 128), 1), 32)
    low = iota((chain_rows, 128), 1) < 64
    result = None
    kept = []
    for k in range(SUPER):
        found = []
        for t in range(tiles):
            tile = None
            for g in range(4):
                yy = 2 * t + g // 2
                source = ss[g % 2, :, 128 * yy:128 * (yy + 1)]
                shift = (32 * (g - k)) % 128
                if shift:
                    source = pltpu.roll(source, shift, 1)
                tile = source if tile is None else jnp.where(quarter == g, source, tile)
            found.append(tile)
        summed = jnp.concatenate(found, axis=1) if tiles > 1 else found[0]
        carried = jnp.zeros_like(summed)
        if k > 0:
            carried = jnp.dot(result, cc[k - 1], preferred_element_type=F32)
            summed = summed + carried
        result = (-(summed * row_mask)).astype(BF16)
        kept.append(jnp.where(h == 0, result.astype(F32), carried))
    for two in range(SUPER // 2):
        for t in range(tiles):
            tile = slice(128 * t, 128 * (t + 1))
            first, second = kept[2 * two][:, tile], kept[2 * two + 1][:, tile]
            lanes = slice(128 * two, 128 * (two + 1))
            zs[2 * t, :, lanes] = jnp.where(low, first, swap_halves(second)).astype(BF16)
            zs[2 * t + 1, :, lanes] = jnp.where(low, swap_halves(first), second).astype(BF16)

    own_rows = pl.ds(pl.multiple_of(chain_rows * y, 16), chain_rows)

    for i in range(1, ny):
        to = mod(y + i, ny)
        remote(zs.at[to], zb.at[own_rows], s_zb, r_zb, dev(x, to, z, h)).start()

    zb[own_rows, :] = zs[y]
    wait_bytes(mw.at[0], r_mf)
    wait_bytes(zb.at[pl.ds(0, chain_rows * (ny - 1))], r_zb)

    @pl.when(h == 0)
    def _():
        remote(zb, zo, s_zo, r_zo, dev(x, y, z, 1)).start()

    low32 = iota((32, 128), 1) < 64
    for k in range(SUPER):
        left = jnp.concatenate(
            [mw[c % 2, c // 2, 32 * k:32 * (k + 1), :] for c in range(2 * ny)], axis=0
        )
        two = k // 2
        product = jnp.dot(
            left, zb[:, 128 * two:128 * (two + 1)], preferred_element_type=F32
        )
        for zz in range(nz):
            upper = product[64 * zz:64 * zz + 32]
            lower = product[64 * zz + 32:64 * zz + 64]
            if k % 2 == 0:
                packed = jnp.where(low32, upper, swap_halves(lower))
            else:
                packed = jnp.where(low32, swap_halves(upper), lower)
            ps[k * nz + zz] = packed.astype(BF16)

    for i in range(1, NX * nz):
        xx, zz = mod(x + i // nz, NX), mod(z + i % nz, nz)
        remote(ps.at[xx * nz + zz], pb.at[i - 1], s_p, r_p, dev(xx, y, zz, h)).start()

    own_lane = 64 * lax.div(iota((128, 256), 0), 32) + 32 * h + lax.rem(iota((128, 256), 0), 32)
    own_lane = jnp.where(iota((128, 256), 1) == own_lane, 1.0, 0.0).astype(BF16)

    def write_panel(source):
        turned = lax.dot_general(own_lane, source[...], NT_DIMS, preferred_element_type=F32)
        outp_ref[...] = turned.astype(BF16).reshape(SUPER, 32, ROWS)

    @pl.when(h == 0)
    def _():
        write_panel(zb)

    @pl.when(h == 1)
    def _():
        wait_bytes(zo, r_zo)
        write_panel(zo)

    wait_bytes(pb, r_p)
    total = ps[x * nz + z].astype(F32)
    for i in range(NX * nz - 1):
        total = total + pb[i].astype(F32)
    ev[...] = jnp.where(h == 0, diag_packed - total, total)

    @pl.when(h == 0)
    def _():
        for i in range(1, ny):
            remote(ev, eb1.at[y], s_e, r_e1, dev(x, mod(y + i, ny), z, 0)).start()
        eb1[y] = ev[...]
        wait_bytes(eb1.at[pl.ds(0, ny - 1)], r_e1)
        remote(eb1, eb1, s_eb, r_e2, dev(x, y, z, 1)).start()

    @pl.when(h == 1)
    def _():
        for i in range(1, ny):
            remote(ev, eb2.at[z], s_e, r_e1, dev(x, mod(y + i, ny), y, 1)).start()

        @pl.when(y == z)
        def _():
            pltpu.make_async_copy(ev, eb2.at[z], r_e1).start()

        @pl.when(y != z)
        def _():
            remote(ev, eb2.at[z], s_e, r_e1, dev(x, y, y, 1)).start()

        wait_bytes(eb2, r_e1)
        remote(eb2, eb2, s_eb, r_e2, dev(x, y, z, 0)).start()

    wait_bytes(eb1, r_e2)
    upper, lower = [], []
    for t in range(tiles):
        first, second = eb1[2 * t], eb1[2 * t + 1]
        upper.append(jnp.where(low32, first, swap_halves(second)))
        lower.append(jnp.where(low32, swap_halves(first), second))
    if tiles > 1:
        upper = jnp.concatenate(upper, axis=1)
        lower = jnp.concatenate(lower, axis=1)
    else:
        upper, lower = upper[0], lower[0]
    straight = jnp.concatenate(split(jnp.concatenate([upper, lower], axis=0)), axis=0)
    stack = []
    for b in range(nz):
        stack += [eb2[b], swap_halves(eb2[b])]
    high, rest = split(jnp.concatenate(stack, axis=0))
    stack = jnp.where(
        iota((width, 128), 1) < 64, high.astype(F32), swap_halves(rest.astype(F32))
    ).astype(BF16)
    right_side = vst[x]
    own = jnp.dot(straight, right_side, preferred_element_type=F32)
    own = own + lax.dot_general(stack, right_side, TN_DIMS, preferred_element_type=F32)
    own = own[0:64] + own[64:128]
    mine_f = fb.at[x * nz + z]
    mine_f[...] = own.astype(BF16)
    order = [(i + 1) // 2 if i % 2 else nz - i // 2 for i in range(1, nz)]
    for delta in order:
        remote(mine_f, mine_f, s_f, frecv.at[delta], dev(x, y, mod(z + delta, nz), h)).start()
    for delta in [0] + order:
        slot = fb.at[x * nz + mod(z - delta, nz)]
        if delta:
            wait_bytes(slot, frecv.at[delta])
        for i in (2, 1, 3):
            remote(slot, slot, s_f, r_f, dev(mod(x + i, NX), y, z, h)).start()
    wait_bytes(fb.at[pl.ds(0, (NX - 1) * nz)], r_f)
    state = fb[pl.ds(0, nz)].reshape(width, 128).astype(F32)
    for j in range(SUPER - 1):
        moved = jnp.dot(
            ct[j], jnp.concatenate(split(state), axis=1), preferred_element_type=F32
        )
        moved = moved[:, 0:128] + moved[:, 128:256]
        added = fb[pl.ds((j + 1) * nz, nz)].reshape(width, 128).astype(F32)
        state = added + jnp.where(group > j, moved, state)
    outd_ref[...] = state.T.reshape(SUPER, 32, width)

    @pl.when(y != z)
    def _():
        wait_bytes(home, s_t)

    wait_bytes(tp.at[0, 0], s_tp)
    wait_bytes(tp.at[0], s_td)
    wait_bytes(dgs, s_dg)
    wait_bytes(ms.at[pl.ds(0, nz - 1)], s_z)
    wait_bytes(mw.at[0, pl.ds(0, ny - 1)], s_mw)
    wait_bytes(ms.at[pl.ds(0, nz)], s_x)
    wait_bytes(got, s_p2)
    wait_bytes(rb, s_rs)
    wait_bytes(mw.at[0], s_mf)
    wait_bytes(ss.at[0], s_ss)
    wait_bytes(zb.at[pl.ds(0, chain_rows * (ny - 1))], s_zb)

    @pl.when(h == 0)
    def _():
        wait_bytes(zo, s_zo)

    wait_bytes(pb, s_p)
    wait_bytes(eb1.at[pl.ds(0, ny - 1)], s_e)
    wait_bytes(eb1, s_eb)

    @pl.when(jnp.logical_and(h == 1, y != z))
    def _():
        wait_bytes(ev, s_e)

    wait_bytes(fb.at[pl.ds(0, nz - 1)], s_f)
    wait_bytes(fb.at[pl.ds(0, (NX - 1) * nz)], s_f)


def on_device(trail_inverse, panels, couplings, diag_terms, listed):
    ny = lax.axis_size("col") // 2
    nz = ny
    width = 64 * ny
    chain_rows = ROWS // ny
    vmem = pl.BlockSpec(memory_space=pltpu.VMEM)
    anywhere = pl.BlockSpec(memory_space=pltpu.HBM)
    panel, diag = pl.pallas_call(
        functools.partial(kernel, ny),
        out_shape=(
            jax.ShapeDtypeStruct((SUPER, 32, ROWS), BF16),
            jax.ShapeDtypeStruct((SUPER, 32, width), F32),
        ),
        in_specs=[vmem, vmem, anywhere, anywhere, anywhere],
        out_specs=(vmem, vmem),
        scratch_shapes=[
            pltpu.VMEM((2, 2, ROWS, ROWS), BF16),
            pltpu.VMEM((SUPER - 1, width, width), BF16),
            pltpu.VMEM((SUPER - 1, width, width), BF16),
            pltpu.VMEM((SUPER, width, 128), BF16),
            pltpu.VMEM((32, 128), F32),
            pltpu.VMEM((32, 128), F32),
            pltpu.VMEM((2, ny, PIECE, ROWS), BF16),
            pltpu.VMEM((nz * NX, PIECE, ROWS), BF16),
            pltpu.VMEM((nz, ROWS, PIECE), F32),
            pltpu.VMEM((nz, ROWS, PIECE), BF16),
            pltpu.VMEM((nz, ROWS, PIECE), BF16),
            pltpu.VMEM((ny, chain_rows, 128 * ny), BF16),
            pltpu.VMEM((ny - 1, chain_rows, 128 * ny), BF16),
            pltpu.VMEM((2, chain_rows, 128 * ny), F32),
            pltpu.VMEM((ny, chain_rows, 256), BF16),
            pltpu.VMEM((ROWS, 256), BF16),
            pltpu.VMEM((ROWS, 256), BF16),
            pltpu.VMEM((NX * nz, 32, 128), BF16),
            pltpu.VMEM((NX * nz - 1, 32, 128), BF16),
            pltpu.VMEM((32, 128), F32),
            pltpu.VMEM((ny, 32, 128), F32),
            pltpu.VMEM((nz, 32, 128), F32),
            pltpu.VMEM((NX * nz, 64, 128), BF16),
            pltpu.SemaphoreType.DMA((34,)),
            pltpu.SemaphoreType.DMA((2, nz)),
            pltpu.SemaphoreType.DMA((2, nz)),
            pltpu.SemaphoreType.DMA((nz,)),
            pltpu.SemaphoreType.DMA((ny,)),
            pltpu.SemaphoreType.DMA((nz,)),
        ],
        compiler_params=pltpu.CompilerParams(
            collective_id=0, has_side_effects=True, vmem_limit_bytes=53 * 1024 * 1024
        ),
        name="chain",
    )(
        panels.swapaxes(1, 2), listed.reshape(1, -1), trail_inverse, couplings,
        diag_terms.swapaxes(1, 2),
    )
    return panel.swapaxes(1, 2), diag.swapaxes(1, 2)


def solution(mesh):
    in_specs = (P("row", "col"), P(None, "row", "col"), P(), P(None, None, "col"), P())
    out_specs = (P(None, "row", "col"), P(None, None, "col"))
    return jax.shard_map(
        on_device, mesh=mesh, in_specs=in_specs, out_specs=out_specs, check_vma=False
    )
```

```python
import functools

import jax
import jax.numpy as jnp
from jax import lax
from jax.experimental import pallas as pl
from jax.experimental.pallas import tpu as pltpu
from jax.sharding import PartitionSpec as P

SUPER = 4
NX = 4
ROWS = 384
PIECE = 128
PARTS = 4
LAG = 3
ADD = 5
MESH = pl.DeviceIdType.MESH
F32 = jnp.float32
BF16 = jnp.bfloat16
NT_DIMS = (((1,), (1,)), ((), ()))
TN_DIMS = (((0,), (0,)), ((), ()))


def iota(shape, dim):
    return lax.broadcasted_iota(jnp.int32, shape, dim)


def mod(value, size):
    value = jnp.where(value < 0, value + size, value)
    return jnp.where(value >= size, value - size, value)


def split(value):
    high = value.astype(BF16)
    return [high, (value - high.astype(F32)).astype(BF16)]


def swap_halves(value):
    return pltpu.roll(value, 64, 1)


def kernel(
    ny,
    panels_ref, listed_ref, trail_ref, coup_ref, diag_ref,
    outp_ref, outd_ref,
    tp, cc, ct, vst, dgo, dgs, mw, ms, held, out, got, sp, rb, ss, zs, zb, zo, ps, pb, ev, eb1, eb2, fb,
    sem, zrecv, xrecv, precv, yrecv, frecv,
):
    nz = ny
    width = 64 * ny
    chain_rows = ROWS // ny
    tiles = width // 128
    row, col = lax.axis_index("row"), lax.axis_index("col")
    z, x = lax.div(row, NX), lax.rem(row, NX)
    y, h = lax.div(col, 2), lax.rem(col, 2)
    sibling = 1 - h

    def dev(xx, yy, zz, hh):
        return (zz * NX + xx, yy * 2 + hh)

    def remote(src, dst, send, recv, device):
        return pltpu.make_async_remote_copy(
            src_ref=src, dst_ref=dst, send_sem=send, recv_sem=recv,
            device_id=device, device_id_type=MESH,
        )

    def wait_bytes(ref, semaphore):
        pltpu.make_async_copy(ref, ref, semaphore).wait()

    (s_t, s_z, s_x, s_mw, s_p2, s_eb, s_td, r_td, s_tp, r_tp, s_rs, r_rs, s_ss, r_ss, s_zb, r_zb,
     s_mf, r_mf, s_zo, r_zo, s_p, r_p, s_e, r_e1, r_e2, s_f, r_f, s_dg, r_dg,
     l_tp, l_cc, l_dg) = [sem.at[i] for i in range(32)]

    barrier = pltpu.get_barrier_semaphore()

    def greet(device):
        pl.semaphore_signal(barrier, inc=1, device_id=device, device_id_type=MESH)

    greet(dev(x, y, z, sibling))
    for step in (1, nz - 1) if nz > 2 else (1,):
        greet(dev(x, y, mod(z + step, nz), h))
    for step in range(1, NX):
        greet(dev(mod(x + step, NX), y, z, h))
    for step in range(1, ny):
        greet(dev(x, mod(y + step, ny), z, h))

    @pl.when(y != z)
    def _():
        greet(dev(x, z, y, h))

    pair = x + 1 - 2 * lax.rem(x, 2)
    inner = jnp.where(jnp.logical_or(x == 1, x == 2), 1, 0)

    def side_of(core):
        return jnp.where(core == inner, 0, 1)

    kept_side, given_side = side_of(h), 1 - side_of(h)
    own_tp = pltpu.make_async_copy(
        trail_ref.at[:, pl.ds(pl.multiple_of(kept_side * ROWS, ROWS), ROWS)], tp.at[h, 0], l_tp
    )
    own_tp.start()
    own_cc = pltpu.make_async_copy(coup_ref, cc, l_cc)
    own_cc.start()
    diag_tile = diag_ref.at[x, :, pl.ds(pl.multiple_of(lax.div(z, 2) * 128, 128), 128)]
    own_dg = pltpu.make_async_copy(diag_tile, dgo, l_dg)
    own_dg.start()

    listed = listed_ref[...]

    def flag(block):
        return jnp.max(jnp.where(listed == block, 1.0, 0.0), axis=1, keepdims=True)

    lane = iota((1, ROWS), 1)
    piece_mask = jnp.where(
        lane < 128, flag(3 * row), jnp.where(lane < 256, flag(3 * row + 1), flag(3 * row + 2))
    )
    for k in range(SUPER):
        turned = panels_ref[k].astype(F32)
        mw[h, y, 32 * k:32 * (k + 1), :] = (turned * piece_mask).astype(BF16)

    pl.semaphore_wait(
        barrier, min(2, nz - 1) + NX + ny - 1 + jnp.where(y != z, 1, 0)
    )

    mine = mw.at[h, y]
    size = PIECE // PARTS
    parts = [pl.ds(size * part, size) for part in range(PARTS)]

    for part in range(PARTS):
        target = ms.at[y * NX + x, parts[part]]

        @pl.when(y != z)
        def _():
            remote(mine.at[parts[part]], target, s_t, zrecv.at[part, 0], dev(x, z, y, h)).start()

        @pl.when(y == z)
        def _():
            pltpu.make_async_copy(mine.at[parts[part]], target, zrecv.at[part, 0]).start()

    given = trail_ref.at[:, pl.ds(pl.multiple_of(given_side * ROWS, ROWS), ROWS)]
    remote(given, tp.at[h, 1], s_tp, r_tp, dev(pair, y, z, h)).start()
    send_dg = remote(diag_tile, dgs, s_dg, r_dg, dev(x, y, z, sibling))
    send_dg.start()

    def near(step):
        half = lax.div(step + 1, 2)
        return jnp.where(lax.rem(step, 2) == 1, half, mod(-half, nz))

    home = ms.at[z * NX + x]

    def relay_piece(step, part):
        slot = ms.at[mod(z - near(step), nz) * NX + x, parts[part]]
        z_next = mod(z + jnp.where(lax.rem(step, 2) == 1, 1, -1), nz)
        wait_bytes(slot, zrecv.at[part, step])

        @pl.when(step == 0)
        def _():
            remote(slot, slot, s_z, zrecv.at[part, 1], dev(x, y, mod(z + 1, nz), h)).start()

        @pl.when(step < nz - 2)
        def _():
            remote(slot, slot, s_z, zrecv.at[part, step + 2], dev(x, y, z_next, h)).start()

        remote(slot, slot, s_x, xrecv.at[part, step], dev(3 - x, y, z, h)).start()

    def relay_wide(step):
        wide = mw.at[h, mod(y - near(step), ny)]
        y_next = mod(y + jnp.where(lax.rem(step, 2) == 1, 1, -1), ny)

        @pl.when(step > 0)
        def _():
            wait_bytes(wide, yrecv.at[step])

        @pl.when(step == 0)
        def _():
            remote(wide, wide, s_mw, yrecv.at[1], dev(x, mod(y + 1, ny), z, h)).start()

        @pl.when(step < ny - 2)
        def _():
            remote(wide, wide, s_mw, yrecv.at[step + 2], dev(x, y_next, z, h)).start()

    @pl.loop(0, nz + ADD)
    def _(step):
        @pl.when(step < nz)
        def _():
            for part in range(PARTS // 2):
                relay_piece(step, part)

        @pl.when(jnp.logical_and(step >= 1, step <= nz))
        def _():
            for part in range(PARTS // 2, PARTS):
                relay_piece(step - 1, part)

        @pl.when(step < nz)
        def _():
            relay_wide(step)

        @pl.when(step == LAG - 2)
        def _():
            own_tp.wait()
            wait_bytes(tp.at[0, 0], r_tp)
            remote(tp.at[h], tp.at[h], s_td, r_td, dev(x, y, z, sibling)).start()

        @pl.when(step == LAG)
        def _():
            wait_bytes(tp.at[0], r_td)

        @pl.when(jnp.logical_and(step >= LAG, step < nz + LAG))
        def _():
            at = step - LAG
            chunk = mod(z - near(at), nz)
            for part in range(PARTS):
                wait_bytes(home.at[parts[part]], xrecv.at[part, at])
            sums = [None, None]
            for core in range(2):
                piece = ms[chunk * NX + 2 * core + side_of(core)]
                for rows in range(2):
                    term = lax.dot_general(
                        tp[core, rows], piece, NT_DIMS, preferred_element_type=F32
                    )
                    sums[rows] = term if core == 0 else sums[rows] + term
            held[chunk] = sums[0]
            out[chunk] = sums[1].astype(BF16)
            remote(out.at[chunk], got.at[chunk], s_p2, precv.at[at], dev(pair, y, z, h)).start()

        @pl.when(step >= ADD)
        def _():
            at = step - ADD
            chunk = mod(z - near(at), nz)
            wait_bytes(got.at[chunk], precv.at[at])
            total = held[chunk] + got[chunk].astype(F32)
            total = total.astype(BF16)
            lanes = pl.ds(pl.multiple_of(chunk * PIECE, PIECE), PIECE)
            for yy in range(ny):
                sp[yy, :, lanes] = total[chain_rows * yy:chain_rows * (yy + 1)]

            for i in range(1, ny):
                to = mod(y + i, ny)
                remote(
                    sp.at[to, :, lanes], rb.at[i - 1, :, lanes], s_rs, r_rs, dev(x, to, z, h)
                ).start()

    send_mf = remote(mw.at[h], mw.at[h], s_mf, r_mf, dev(x, y, z, sibling))
    send_mf.start()

    own_cc.wait()
    wide_eye = jnp.where(iota((width, width), 0) == iota((width, width), 1), 1.0, 0.0)
    wide_eye = wide_eye.astype(BF16)
    group = lax.div(iota((width, 128), 1), 32)
    picks = iota((width, 128), 0) == col * 32 + lax.rem(iota((width, 128), 1), 32)
    for j in range(SUPER - 1):
        ct[j] = lax.dot_general(
            wide_eye, cc[j], NT_DIMS, preferred_element_type=F32
        ).astype(BF16)
    above = None
    for j in reversed(range(SUPER)):
        chosen = jnp.where(jnp.logical_and(picks, group == j), 1.0, 0.0)
        if above is not None:
            chosen = chosen + jnp.dot(cc[j], above, preferred_element_type=F32)
        above = chosen.astype(BF16)
        vst[j] = above

    own_dg.wait()
    wait_bytes(dgs, r_dg)
    both = jnp.concatenate([dgo[...], dgs[...], jnp.zeros((64, 128), F32)], axis=0)
    both = jnp.where(lax.rem(z, 2) == 0, both, swap_halves(both)).T
    diag_packed = jnp.where(iota((32, 128), 1) < 64, both[0:32], swap_halves(both[32:64]))

    wait_bytes(rb, r_rs)
    for t in range(ny):
        lanes = slice(128 * t, 128 * (t + 1))
        total = sp[y, :, lanes].astype(F32)
        for i in range(ny - 1):
            total = total + rb[i, :, lanes].astype(F32)
        ss[h, :, lanes] = total
    send_ss = remote(ss.at[h], ss.at[h], s_ss, r_ss, dev(x, y, z, sibling))
    send_ss.start()
    wait_bytes(ss.at[0], r_ss)

    block = lax.shift_right_logical(
        ROWS * row + chain_rows * y + iota((chain_rows, 1), 0), 7
    )
    row_mask = jnp.max(jnp.where(listed == block, 1.0, 0.0), axis=1, keepdims=True)
    quarter = lax.div(iota((chain_rows, 128), 1), 32)
    low = iota((chain_rows, 128), 1) < 64
    result = None
    kept = []
    for k in range(SUPER):
        found = []
        for t in range(tiles):
            tile = None
            for g in range(4):
                yy = 2 * t + g // 2
                source = ss[g % 2, :, 128 * yy:128 * (yy + 1)]
                shift = (32 * (g - k)) % 128
                if shift:
                    source = pltpu.roll(source, shift, 1)
                tile = source if tile is None else jnp.where(quarter == g, source, tile)
            found.append(tile)
        summed = jnp.concatenate(found, axis=1) if tiles > 1 else found[0]
        carried = jnp.zeros_like(summed)
        if k > 0:
            carried = jnp.dot(result, cc[k - 1], preferred_element_type=F32)
            summed = summed + carried
        result = (-(summed * row_mask)).astype(BF16)
        kept.append(jnp.where(h == 0, result.astype(F32), carried))
    for two in range(SUPER // 2):
        for t in range(tiles):
            tile = slice(128 * t, 128 * (t + 1))
            first, second = kept[2 * two][:, tile], kept[2 * two + 1][:, tile]
            lanes = slice(128 * two, 128 * (two + 1))
            zs[2 * t, :, lanes] = jnp.where(low, first, swap_halves(second)).astype(BF16)
            zs[2 * t + 1, :, lanes] = jnp.where(low, swap_halves(first), second).astype(BF16)

    own_rows = pl.ds(pl.multiple_of(chain_rows * y, 16), chain_rows)

    for i in range(1, ny):
        to = mod(y + i, ny)
        remote(zs.at[to], zb.at[own_rows], s_zb, r_zb, dev(x, to, z, h)).start()

    zb[own_rows, :] = zs[y]
    wait_bytes(mw.at[0], r_mf)
    wait_bytes(zb.at[pl.ds(0, chain_rows * (ny - 1))], r_zb)

    @pl.when(h == 0)
    def _():
        remote(zb, zo, s_zo, r_zo, dev(x, y, z, 1)).start()

    low32 = iota((32, 128), 1) < 64
    for k in range(SUPER):
        left = jnp.concatenate(
            [mw[c % 2, c // 2, 32 * k:32 * (k + 1), :] for c in range(2 * ny)], axis=0
        )
        two = k // 2
        product = jnp.dot(
            left, zb[:, 128 * two:128 * (two + 1)], preferred_element_type=F32
        )
        for zz in range(nz):
            upper = product[64 * zz:64 * zz + 32]
            lower = product[64 * zz + 32:64 * zz + 64]
            if k % 2 == 0:
                packed = jnp.where(low32, upper, swap_halves(lower))
            else:
                packed = jnp.where(low32, swap_halves(upper), lower)
            ps[k * nz + zz] = packed.astype(BF16)

    far_first = sorted(
        range(1, NX * nz),
        key=lambda i: (-min(i % nz, nz - i % nz), -min(i // nz, NX - i // nz), i),
    )
    for i in far_first:
        xx, zz = mod(x + i // nz, NX), mod(z + i % nz, nz)
        remote(ps.at[xx * nz + zz], pb.at[i - 1], s_p, r_p, dev(xx, y, zz, h)).start()

    own_lane = 64 * lax.div(iota((128, 256), 0), 32) + 32 * h + lax.rem(iota((128, 256), 0), 32)
    own_lane = jnp.where(iota((128, 256), 1) == own_lane, 1.0, 0.0).astype(BF16)

    def write_panel(source):
        turned = lax.dot_general(own_lane, source[...], NT_DIMS, preferred_element_type=F32)
        outp_ref[...] = turned.astype(BF16).reshape(SUPER, 32, ROWS)

    @pl.when(h == 0)
    def _():
        write_panel(zb)

    @pl.when(h == 1)
    def _():
        wait_bytes(zo, r_zo)
        write_panel(zo)

    wait_bytes(pb, r_p)
    total = ps[x * nz + z].astype(F32)
    for i in range(NX * nz - 1):
        total = total + pb[i].astype(F32)
    ev[...] = jnp.where(h == 0, diag_packed - total, total)

    @pl.when(h == 0)
    def _():
        for i in range(1, ny):
            remote(ev, eb1.at[y], s_e, r_e1, dev(x, mod(y + i, ny), z, 0)).start()
        eb1[y] = ev[...]
        wait_bytes(eb1.at[pl.ds(0, ny - 1)], r_e1)
        remote(eb1, eb1, s_eb, r_e2, dev(x, y, z, 1)).start()

    @pl.when(h == 1)
    def _():
        for i in range(1, ny):
            remote(ev, eb2.at[z], s_e, r_e1, dev(x, mod(y + i, ny), y, 1)).start()

        @pl.when(y == z)
        def _():
            pltpu.make_async_copy(ev, eb2.at[z], r_e1).start()

        @pl.when(y != z)
        def _():
            remote(ev, eb2.at[z], s_e, r_e1, dev(x, y, y, 1)).start()

        wait_bytes(eb2, r_e1)
        remote(eb2, eb2, s_eb, r_e2, dev(x, y, z, 0)).start()

    wait_bytes(eb1, r_e2)
    upper, lower = [], []
    for t in range(tiles):
        first, second = eb1[2 * t], eb1[2 * t + 1]
        upper.append(jnp.where(low32, first, swap_halves(second)))
        lower.append(jnp.where(low32, swap_halves(first), second))
    if tiles > 1:
        upper = jnp.concatenate(upper, axis=1)
        lower = jnp.concatenate(lower, axis=1)
    else:
        upper, lower = upper[0], lower[0]
    straight = jnp.concatenate(split(jnp.concatenate([upper, lower], axis=0)), axis=0)
    stack = []
    for b in range(nz):
        stack += [eb2[b], swap_halves(eb2[b])]
    high, rest = split(jnp.concatenate(stack, axis=0))
    stack = jnp.where(
        iota((width, 128), 1) < 64, high.astype(F32), swap_halves(rest.astype(F32))
    ).astype(BF16)
    right_side = vst[x]
    own = jnp.dot(straight, right_side, preferred_element_type=F32)
    own = own + lax.dot_general(stack, right_side, TN_DIMS, preferred_element_type=F32)
    own = own[0:64] + own[64:128]
    mine_f = fb.at[x * nz + z]
    mine_f[...] = own.astype(BF16)
    order = [(i + 1) // 2 if i % 2 else nz - i // 2 for i in range(1, nz)]
    for delta in order:
        remote(mine_f, mine_f, s_f, frecv.at[delta], dev(x, y, mod(z + delta, nz), h)).start()
    for delta in [0] + order:
        slot = fb.at[x * nz + mod(z - delta, nz)]
        if delta:
            wait_bytes(slot, frecv.at[delta])
        for i in (2, 1, 3):
            remote(slot, slot, s_f, r_f, dev(mod(x + i, NX), y, z, h)).start()
    wait_bytes(fb.at[pl.ds(0, (NX - 1) * nz)], r_f)
    state = fb[pl.ds(0, nz)].reshape(width, 128).astype(F32)
    for j in range(SUPER - 1):
        moved = jnp.dot(
            ct[j], jnp.concatenate(split(state), axis=1), preferred_element_type=F32
        )
        moved = moved[:, 0:128] + moved[:, 128:256]
        added = fb[pl.ds((j + 1) * nz, nz)].reshape(width, 128).astype(F32)
        state = added + jnp.where(group > j, moved, state)
    outd_ref[...] = state.T.reshape(SUPER, 32, width)

    @pl.when(y != z)
    def _():
        wait_bytes(home, s_t)

    wait_bytes(tp.at[0, 0], s_tp)
    wait_bytes(tp.at[0], s_td)
    wait_bytes(dgs, s_dg)
    wait_bytes(ms.at[pl.ds(0, nz - 1)], s_z)
    wait_bytes(mw.at[0, pl.ds(0, ny - 1)], s_mw)
    wait_bytes(ms.at[pl.ds(0, nz)], s_x)
    wait_bytes(got, s_p2)
    wait_bytes(rb, s_rs)
    wait_bytes(mw.at[0], s_mf)
    wait_bytes(ss.at[0], s_ss)
    wait_bytes(zb.at[pl.ds(0, chain_rows * (ny - 1))], s_zb)

    @pl.when(h == 0)
    def _():
        wait_bytes(zo, s_zo)

    wait_bytes(pb, s_p)
    wait_bytes(eb1.at[pl.ds(0, ny - 1)], s_e)
    wait_bytes(eb1, s_eb)

    @pl.when(jnp.logical_and(h == 1, y != z))
    def _():
        wait_bytes(ev, s_e)

    wait_bytes(fb.at[pl.ds(0, nz - 1)], s_f)
    wait_bytes(fb.at[pl.ds(0, (NX - 1) * nz)], s_f)


def on_device(trail_inverse, panels, couplings, diag_terms, listed):
    ny = lax.axis_size("col") // 2
    nz = ny
    width = 64 * ny
    chain_rows = ROWS // ny
    vmem = pl.BlockSpec(memory_space=pltpu.VMEM)
    anywhere = pl.BlockSpec(memory_space=pltpu.HBM)
    panel, diag = pl.pallas_call(
        functools.partial(kernel, ny),
        out_shape=(
            jax.ShapeDtypeStruct((SUPER, 32, ROWS), BF16),
            jax.ShapeDtypeStruct((SUPER, 32, width), F32),
        ),
        in_specs=[vmem, vmem, anywhere, anywhere, anywhere],
        out_specs=(vmem, vmem),
        scratch_shapes=[
            pltpu.VMEM((2, 2, ROWS, ROWS), BF16),
            pltpu.VMEM((SUPER - 1, width, width), BF16),
            pltpu.VMEM((SUPER - 1, width, width), BF16),
            pltpu.VMEM((SUPER, width, 128), BF16),
            pltpu.VMEM((32, 128), F32),
            pltpu.VMEM((32, 128), F32),
            pltpu.VMEM((2, ny, PIECE, ROWS), BF16),
            pltpu.VMEM((nz * NX, PIECE, ROWS), BF16),
            pltpu.VMEM((nz, ROWS, PIECE), F32),
            pltpu.VMEM((nz, ROWS, PIECE), BF16),
            pltpu.VMEM((nz, ROWS, PIECE), BF16),
            pltpu.VMEM((ny, chain_rows, 128 * ny), BF16),
            pltpu.VMEM((ny - 1, chain_rows, 128 * ny), BF16),
            pltpu.VMEM((2, chain_rows, 128 * ny), F32),
            pltpu.VMEM((ny, chain_rows, 256), BF16),
            pltpu.VMEM((ROWS, 256), BF16),
            pltpu.VMEM((ROWS, 256), BF16),
            pltpu.VMEM((NX * nz, 32, 128), BF16),
            pltpu.VMEM((NX * nz - 1, 32, 128), BF16),
            pltpu.VMEM((32, 128), F32),
            pltpu.VMEM((ny, 32, 128), F32),
            pltpu.VMEM((nz, 32, 128), F32),
            pltpu.VMEM((NX * nz, 64, 128), BF16),
            pltpu.SemaphoreType.DMA((32,)),
            pltpu.SemaphoreType.DMA((PARTS, nz)),
            pltpu.SemaphoreType.DMA((PARTS, nz)),
            pltpu.SemaphoreType.DMA((nz,)),
            pltpu.SemaphoreType.DMA((ny,)),
            pltpu.SemaphoreType.DMA((nz,)),
        ],
        compiler_params=pltpu.CompilerParams(
            collective_id=0, has_side_effects=True, vmem_limit_bytes=53 * 1024 * 1024
        ),
        name="chain",
    )(
        panels.swapaxes(1, 2), listed.reshape(1, -1), trail_inverse, couplings,
        diag_terms.swapaxes(1, 2),
    )
    return panel.swapaxes(1, 2), diag.swapaxes(1, 2)


def solution(mesh):
    in_specs = (P("row", "col"), P(None, "row", "col"), P(), P(None, None, "col"), P())
    out_specs = (P(None, "row", "col"), P(None, None, "col"))
    return jax.shard_map(
        on_device, mesh=mesh, in_specs=in_specs, out_specs=out_specs, check_vma=False
    )
```

```python
import functools

import jax
import jax.numpy as jnp
from jax import lax
from jax.experimental import pallas as pl
from jax.experimental.pallas import tpu as pltpu
from jax.sharding import PartitionSpec as P

SUPER = 4
NX = 4
ROWS = 384
PIECE = 128
PARTS = 4
LAG = 2
ADD = 4
MESH = pl.DeviceIdType.MESH
F32 = jnp.float32
BF16 = jnp.bfloat16
NT_DIMS = (((1,), (1,)), ((), ()))
TN_DIMS = (((0,), (0,)), ((), ()))


def iota(shape, dim):
    return lax.broadcasted_iota(jnp.int32, shape, dim)


def mod(value, size):
    value = jnp.where(value < 0, value + size, value)
    return jnp.where(value >= size, value - size, value)


def split(value):
    high = value.astype(BF16)
    return [high, (value - high.astype(F32)).astype(BF16)]


def swap_halves(value):
    return pltpu.roll(value, 64, 1)


def kernel(
    ny,
    panels_ref, listed_ref, trail_ref, coup_ref, diag_ref,
    outp_ref, outd_ref,
    tp, cc, ct, vst, dgo, dgs, mw, ms, held, out, got, sp, rb, ss, zs, zb, zo, ps, pb, ev, eb1, eb2, fb,
    sem, zrecv, xrecv, precv, yrecv, frecv,
):
    nz = ny
    width = 64 * ny
    chain_rows = ROWS // ny
    tiles = width // 128
    row, col = lax.axis_index("row"), lax.axis_index("col")
    z, x = lax.div(row, NX), lax.rem(row, NX)
    y, h = lax.div(col, 2), lax.rem(col, 2)
    sibling = 1 - h

    def dev(xx, yy, zz, hh):
        return (zz * NX + xx, yy * 2 + hh)

    def remote(src, dst, send, recv, device):
        return pltpu.make_async_remote_copy(
            src_ref=src, dst_ref=dst, send_sem=send, recv_sem=recv,
            device_id=device, device_id_type=MESH,
        )

    def wait_bytes(ref, semaphore):
        pltpu.make_async_copy(ref, ref, semaphore).wait()

    (s_t, s_z, s_x, s_mw, s_p2, s_eb, s_td, r_td, s_tp, r_tp, s_rs, r_rs, s_ss, r_ss, s_zb, r_zb,
     s_mf, r_mf, s_zo, r_zo, s_p, r_p, s_e, r_e1, r_e2, s_f, r_f, s_dg, r_dg,
     l_tp, l_cc, l_dg) = [sem.at[i] for i in range(32)]

    barrier = pltpu.get_barrier_semaphore()

    def greet(device):
        pl.semaphore_signal(barrier, inc=1, device_id=device, device_id_type=MESH)

    greet(dev(x, y, z, sibling))
    for step in (1, nz - 1) if nz > 2 else (1,):
        greet(dev(x, y, mod(z + step, nz), h))
    for step in range(1, NX):
        greet(dev(mod(x + step, NX), y, z, h))
    for step in range(1, ny):
        greet(dev(x, mod(y + step, ny), z, h))

    @pl.when(y != z)
    def _():
        greet(dev(x, z, y, h))

    pair = x + 1 - 2 * lax.rem(x, 2)
    inner = jnp.where(jnp.logical_or(x == 1, x == 2), 1, 0)

    def side_of(core):
        return jnp.where(core == inner, 0, 1)

    kept_side, given_side = side_of(h), 1 - side_of(h)
    own_tp = pltpu.make_async_copy(
        trail_ref.at[:, pl.ds(pl.multiple_of(kept_side * ROWS, ROWS), ROWS)], tp.at[h, 0], l_tp
    )
    own_tp.start()
    own_cc = pltpu.make_async_copy(coup_ref, cc, l_cc)
    own_cc.start()
    diag_tile = diag_ref.at[x, :, pl.ds(pl.multiple_of(lax.div(z, 2) * 128, 128), 128)]
    own_dg = pltpu.make_async_copy(diag_tile, dgo, l_dg)
    own_dg.start()

    listed = listed_ref[...]

    def flag(block):
        return jnp.max(jnp.where(listed == block, 1.0, 0.0), axis=1, keepdims=True)

    lane = iota((1, ROWS), 1)
    piece_mask = jnp.where(
        lane < 128, flag(3 * row), jnp.where(lane < 256, flag(3 * row + 1), flag(3 * row + 2))
    )
    for k in range(SUPER):
        turned = panels_ref[k].astype(F32)
        mw[h, y, 32 * k:32 * (k + 1), :] = (turned * piece_mask).astype(BF16)

    pl.semaphore_wait(
        barrier, min(2, nz - 1) + NX + ny - 1 + jnp.where(y != z, 1, 0)
    )

    mine = mw.at[h, y]
    size = PIECE // PARTS
    parts = [pl.ds(size * part, size) for part in range(PARTS)]

    for part in range(PARTS):
        target = ms.at[y * NX + x, parts[part]]

        @pl.when(y != z)
        def _():
            remote(mine.at[parts[part]], target, s_t, zrecv.at[part, 0], dev(x, z, y, h)).start()

        @pl.when(y == z)
        def _():
            pltpu.make_async_copy(mine.at[parts[part]], target, zrecv.at[part, 0]).start()

    given = trail_ref.at[:, pl.ds(pl.multiple_of(given_side * ROWS, ROWS), ROWS)]
    remote(given, tp.at[h, 1], s_tp, r_tp, dev(pair, y, z, h)).start()
    send_dg = remote(diag_tile, dgs, s_dg, r_dg, dev(x, y, z, sibling))
    send_dg.start()

    def near(step):
        half = lax.div(step + 1, 2)
        return jnp.where(lax.rem(step, 2) == 1, half, mod(-half, nz))

    home = ms.at[z * NX + x]

    def relay_piece(step, part):
        slot = ms.at[mod(z - near(step), nz) * NX + x, parts[part]]
        z_next = mod(z + jnp.where(lax.rem(step, 2) == 1, 1, -1), nz)
        wait_bytes(slot, zrecv.at[part, step])

        @pl.when(step == 0)
        def _():
            remote(slot, slot, s_z, zrecv.at[part, 1], dev(x, y, mod(z + 1, nz), h)).start()

        @pl.when(step < nz - 2)
        def _():
            remote(slot, slot, s_z, zrecv.at[part, step + 2], dev(x, y, z_next, h)).start()

        remote(slot, slot, s_x, xrecv.at[part, step], dev(3 - x, y, z, h)).start()

    def relay_wide(step):
        wide = mw.at[h, mod(y - near(step), ny)]
        y_next = mod(y + jnp.where(lax.rem(step, 2) == 1, 1, -1), ny)

        @pl.when(step > 0)
        def _():
            wait_bytes(wide, yrecv.at[step])

        @pl.when(step == 0)
        def _():
            remote(wide, wide, s_mw, yrecv.at[1], dev(x, mod(y + 1, ny), z, h)).start()

        @pl.when(step < ny - 2)
        def _():
            remote(wide, wide, s_mw, yrecv.at[step + 2], dev(x, y_next, z, h)).start()

    @pl.loop(0, nz + ADD)
    def _(step):
        @pl.when(step < nz)
        def _():
            for part in range(PARTS):
                relay_piece(step, part)

        @pl.when(step < nz)
        def _():
            relay_wide(step)

        @pl.when(step == LAG - 2)
        def _():
            own_tp.wait()
            wait_bytes(tp.at[0, 0], r_tp)
            remote(tp.at[h], tp.at[h], s_td, r_td, dev(x, y, z, sibling)).start()

        @pl.when(step == LAG)
        def _():
            wait_bytes(tp.at[0], r_td)

        @pl.when(jnp.logical_and(step >= LAG, step < nz + LAG))
        def _():
            at = step - LAG
            chunk = mod(z - near(at), nz)
            for part in range(PARTS):
                wait_bytes(home.at[parts[part]], xrecv.at[part, at])
            sums = [None, None]
            for core in range(2):
                piece = ms[chunk * NX + 2 * core + side_of(core)]
                for rows in range(2):
                    term = lax.dot_general(
                        tp[core, rows], piece, NT_DIMS, preferred_element_type=F32
                    )
                    sums[rows] = term if core == 0 else sums[rows] + term
            held[chunk] = sums[0]
            out[chunk] = sums[1].astype(BF16)
            remote(out.at[chunk], got.at[chunk], s_p2, precv.at[at], dev(pair, y, z, h)).start()

        @pl.when(step >= ADD)
        def _():
            at = step - ADD
            chunk = mod(z - near(at), nz)
            wait_bytes(got.at[chunk], precv.at[at])
            total = held[chunk] + got[chunk].astype(F32)
            total = total.astype(BF16)
            lanes = pl.ds(pl.multiple_of(chunk * PIECE, PIECE), PIECE)
            for yy in range(ny):
                sp[yy, :, lanes] = total[chain_rows * yy:chain_rows * (yy + 1)]

            for i in range(1, ny):
                to = mod(y + i, ny)
                remote(
                    sp.at[to, :, lanes], rb.at[i - 1, :, lanes], s_rs, r_rs, dev(x, to, z, h)
                ).start()

    send_mf = remote(mw.at[h], mw.at[h], s_mf, r_mf, dev(x, y, z, sibling))
    send_mf.start()

    own_cc.wait()
    wide_eye = jnp.where(iota((width, width), 0) == iota((width, width), 1), 1.0, 0.0)
    wide_eye = wide_eye.astype(BF16)
    group = lax.div(iota((width, 128), 1), 32)
    picks = iota((width, 128), 0) == col * 32 + lax.rem(iota((width, 128), 1), 32)
    for j in range(SUPER - 1):
        ct[j] = lax.dot_general(
            wide_eye, cc[j], NT_DIMS, preferred_element_type=F32
        ).astype(BF16)
    above = None
    for j in reversed(range(SUPER)):
        chosen = jnp.where(jnp.logical_and(picks, group == j), 1.0, 0.0)
        if above is not None:
            chosen = chosen + jnp.dot(cc[j], above, preferred_element_type=F32)
        above = chosen.astype(BF16)
        vst[j] = above

    own_dg.wait()
    wait_bytes(dgs, r_dg)
    both = jnp.concatenate([dgo[...], dgs[...], jnp.zeros((64, 128), F32)], axis=0)
    both = jnp.where(lax.rem(z, 2) == 0, both, swap_halves(both)).T
    diag_packed = jnp.where(iota((32, 128), 1) < 64, both[0:32], swap_halves(both[32:64]))

    wait_bytes(rb, r_rs)
    for t in range(ny):
        lanes = slice(128 * t, 128 * (t + 1))
        total = sp[y, :, lanes].astype(F32)
        for i in range(ny - 1):
            total = total + rb[i, :, lanes].astype(F32)
        ss[h, :, lanes] = total
    send_ss = remote(ss.at[h], ss.at[h], s_ss, r_ss, dev(x, y, z, sibling))
    send_ss.start()
    wait_bytes(ss.at[0], r_ss)

    block = lax.shift_right_logical(
        ROWS * row + chain_rows * y + iota((chain_rows, 1), 0), 7
    )
    row_mask = jnp.max(jnp.where(listed == block, 1.0, 0.0), axis=1, keepdims=True)
    quarter = lax.div(iota((chain_rows, 128), 1), 32)
    low = iota((chain_rows, 128), 1) < 64
    result = None
    kept = []
    for k in range(SUPER):
        found = []
        for t in range(tiles):
            tile = None
            for g in range(4):
                yy = 2 * t + g // 2
                source = ss[g % 2, :, 128 * yy:128 * (yy + 1)]
                shift = (32 * (g - k)) % 128
                if shift:
                    source = pltpu.roll(source, shift, 1)
                tile = source if tile is None else jnp.where(quarter == g, source, tile)
            found.append(tile)
        summed = jnp.concatenate(found, axis=1) if tiles > 1 else found[0]
        carried = jnp.zeros_like(summed)
        if k > 0:
            carried = jnp.dot(result, cc[k - 1], preferred_element_type=F32)
            summed = summed + carried
        result = (-(summed * row_mask)).astype(BF16)
        kept.append(jnp.where(h == 0, result.astype(F32), carried))
    for two in range(SUPER // 2):
        for t in range(tiles):
            tile = slice(128 * t, 128 * (t + 1))
            first, second = kept[2 * two][:, tile], kept[2 * two + 1][:, tile]
            lanes = slice(128 * two, 128 * (two + 1))
            zs[2 * t, :, lanes] = jnp.where(low, first, swap_halves(second)).astype(BF16)
            zs[2 * t + 1, :, lanes] = jnp.where(low, swap_halves(first), second).astype(BF16)

    own_rows = pl.ds(pl.multiple_of(chain_rows * y, 16), chain_rows)

    for i in range(1, ny):
        to = mod(y + i, ny)
        remote(zs.at[to], zb.at[own_rows], s_zb, r_zb, dev(x, to, z, h)).start()

    zb[own_rows, :] = zs[y]
    wait_bytes(mw.at[0], r_mf)
    wait_bytes(zb.at[pl.ds(0, chain_rows * (ny - 1))], r_zb)

    @pl.when(h == 0)
    def _():
        remote(zb, zo, s_zo, r_zo, dev(x, y, z, 1)).start()

    low32 = iota((32, 128), 1) < 64
    for k in range(SUPER):
        left = jnp.concatenate(
            [mw[c % 2, c // 2, 32 * k:32 * (k + 1), :] for c in range(2 * ny)], axis=0
        )
        two = k // 2
        product = jnp.dot(
            left, zb[:, 128 * two:128 * (two + 1)], preferred_element_type=F32
        )
        for zz in range(nz):
            upper = product[64 * zz:64 * zz + 32]
            lower = product[64 * zz + 32:64 * zz + 64]
            if k % 2 == 0:
                packed = jnp.where(low32, upper, swap_halves(lower))
            else:
                packed = jnp.where(low32, swap_halves(upper), lower)
            ps[k * nz + zz] = packed.astype(BF16)

    far_first = sorted(
        range(1, NX * nz),
        key=lambda i: (-min(i % nz, nz - i % nz), -min(i // nz, NX - i // nz), i),
    )
    for i in far_first:
        xx, zz = mod(x + i // nz, NX), mod(z + i % nz, nz)
        remote(ps.at[xx * nz + zz], pb.at[i - 1], s_p, r_p, dev(xx, y, zz, h)).start()

    own_lane = 64 * lax.div(iota((128, 256), 0), 32) + 32 * h + lax.rem(iota((128, 256), 0), 32)
    own_lane = jnp.where(iota((128, 256), 1) == own_lane, 1.0, 0.0).astype(BF16)

    def write_panel(source):
        turned = lax.dot_general(own_lane, source[...], NT_DIMS, preferred_element_type=F32)
        outp_ref[...] = turned.astype(BF16).reshape(SUPER, 32, ROWS)

    @pl.when(h == 0)
    def _():
        write_panel(zb)

    @pl.when(h == 1)
    def _():
        wait_bytes(zo, r_zo)
        write_panel(zo)

    wait_bytes(pb, r_p)
    total = ps[x * nz + z].astype(F32)
    for i in range(NX * nz - 1):
        total = total + pb[i].astype(F32)
    ev[...] = jnp.where(h == 0, diag_packed - total, total)

    @pl.when(h == 0)
    def _():
        for i in range(1, ny):
            remote(ev, eb1.at[y], s_e, r_e1, dev(x, mod(y + i, ny), z, 0)).start()
        eb1[y] = ev[...]
        wait_bytes(eb1.at[pl.ds(0, ny - 1)], r_e1)
        remote(eb1, eb1, s_eb, r_e2, dev(x, y, z, 1)).start()

    @pl.when(h == 1)
    def _():
        for i in range(1, ny):
            remote(ev, eb2.at[z], s_e, r_e1, dev(x, mod(y + i, ny), y, 1)).start()

        @pl.when(y == z)
        def _():
            pltpu.make_async_copy(ev, eb2.at[z], r_e1).start()

        @pl.when(y != z)
        def _():
            remote(ev, eb2.at[z], s_e, r_e1, dev(x, y, y, 1)).start()

        wait_bytes(eb2, r_e1)
        remote(eb2, eb2, s_eb, r_e2, dev(x, y, z, 0)).start()

    wait_bytes(eb1, r_e2)
    upper, lower = [], []
    for t in range(tiles):
        first, second = eb1[2 * t], eb1[2 * t + 1]
        upper.append(jnp.where(low32, first, swap_halves(second)))
        lower.append(jnp.where(low32, swap_halves(first), second))
    if tiles > 1:
        upper = jnp.concatenate(upper, axis=1)
        lower = jnp.concatenate(lower, axis=1)
    else:
        upper, lower = upper[0], lower[0]
    straight = jnp.concatenate(split(jnp.concatenate([upper, lower], axis=0)), axis=0)
    stack = []
    for b in range(nz):
        stack += [eb2[b], swap_halves(eb2[b])]
    high, rest = split(jnp.concatenate(stack, axis=0))
    stack = jnp.where(
        iota((width, 128), 1) < 64, high.astype(F32), swap_halves(rest.astype(F32))
    ).astype(BF16)
    right_side = vst[x]
    own = jnp.dot(straight, right_side, preferred_element_type=F32)
    own = own + lax.dot_general(stack, right_side, TN_DIMS, preferred_element_type=F32)
    own = own[0:64] + own[64:128]
    mine_f = fb.at[x * nz + z]
    mine_f[...] = own.astype(BF16)
    order = [(i + 1) // 2 if i % 2 else nz - i // 2 for i in range(1, nz)]
    for delta in order:
        remote(mine_f, mine_f, s_f, frecv.at[delta], dev(x, y, mod(z + delta, nz), h)).start()
    for delta in [0] + order:
        slot = fb.at[x * nz + mod(z - delta, nz)]
        if delta:
            wait_bytes(slot, frecv.at[delta])
        for i in (2, 1, 3):
            remote(slot, slot, s_f, r_f, dev(mod(x + i, NX), y, z, h)).start()
    wait_bytes(fb.at[pl.ds(0, (NX - 1) * nz)], r_f)
    state = fb[pl.ds(0, nz)].reshape(width, 128).astype(F32)
    for j in range(SUPER - 1):
        moved = jnp.dot(
            ct[j], jnp.concatenate(split(state), axis=1), preferred_element_type=F32
        )
        moved = moved[:, 0:128] + moved[:, 128:256]
        added = fb[pl.ds((j + 1) * nz, nz)].reshape(width, 128).astype(F32)
        state = added + jnp.where(group > j, moved, state)
    outd_ref[...] = state.T.reshape(SUPER, 32, width)

    @pl.when(y != z)
    def _():
        wait_bytes(home, s_t)

    wait_bytes(tp.at[0, 0], s_tp)
    wait_bytes(tp.at[0], s_td)
    wait_bytes(dgs, s_dg)
    wait_bytes(ms.at[pl.ds(0, nz - 1)], s_z)
    wait_bytes(mw.at[0, pl.ds(0, ny - 1)], s_mw)
    wait_bytes(ms.at[pl.ds(0, nz)], s_x)
    wait_bytes(got, s_p2)
    wait_bytes(rb, s_rs)
    wait_bytes(mw.at[0], s_mf)
    wait_bytes(ss.at[0], s_ss)
    wait_bytes(zb.at[pl.ds(0, chain_rows * (ny - 1))], s_zb)

    @pl.when(h == 0)
    def _():
        wait_bytes(zo, s_zo)

    wait_bytes(pb, s_p)
    wait_bytes(eb1.at[pl.ds(0, ny - 1)], s_e)
    wait_bytes(eb1, s_eb)

    @pl.when(jnp.logical_and(h == 1, y != z))
    def _():
        wait_bytes(ev, s_e)

    wait_bytes(fb.at[pl.ds(0, nz - 1)], s_f)
    wait_bytes(fb.at[pl.ds(0, (NX - 1) * nz)], s_f)


def on_device(trail_inverse, panels, couplings, diag_terms, listed):
    ny = lax.axis_size("col") // 2
    nz = ny
    width = 64 * ny
    chain_rows = ROWS // ny
    vmem = pl.BlockSpec(memory_space=pltpu.VMEM)
    anywhere = pl.BlockSpec(memory_space=pltpu.HBM)
    panel, diag = pl.pallas_call(
        functools.partial(kernel, ny),
        out_shape=(
            jax.ShapeDtypeStruct((SUPER, 32, ROWS), BF16),
            jax.ShapeDtypeStruct((SUPER, 32, width), F32),
        ),
        in_specs=[vmem, vmem, anywhere, anywhere, anywhere],
        out_specs=(vmem, vmem),
        scratch_shapes=[
            pltpu.VMEM((2, 2, ROWS, ROWS), BF16),
            pltpu.VMEM((SUPER - 1, width, width), BF16),
            pltpu.VMEM((SUPER - 1, width, width), BF16),
            pltpu.VMEM((SUPER, width, 128), BF16),
            pltpu.VMEM((32, 128), F32),
            pltpu.VMEM((32, 128), F32),
            pltpu.VMEM((2, ny, PIECE, ROWS), BF16),
            pltpu.VMEM((nz * NX, PIECE, ROWS), BF16),
            pltpu.VMEM((nz, ROWS, PIECE), F32),
            pltpu.VMEM((nz, ROWS, PIECE), BF16),
            pltpu.VMEM((nz, ROWS, PIECE), BF16),
            pltpu.VMEM((ny, chain_rows, 128 * ny), BF16),
            pltpu.VMEM((ny - 1, chain_rows, 128 * ny), BF16),
            pltpu.VMEM((2, chain_rows, 128 * ny), F32),
            pltpu.VMEM((ny, chain_rows, 256), BF16),
            pltpu.VMEM((ROWS, 256), BF16),
            pltpu.VMEM((ROWS, 256), BF16),
            pltpu.VMEM((NX * nz, 32, 128), BF16),
            pltpu.VMEM((NX * nz - 1, 32, 128), BF16),
            pltpu.VMEM((32, 128), F32),
            pltpu.VMEM((ny, 32, 128), F32),
            pltpu.VMEM((nz, 32, 128), F32),
            pltpu.VMEM((NX * nz, 64, 128), BF16),
            pltpu.SemaphoreType.DMA((32,)),
            pltpu.SemaphoreType.DMA((PARTS, nz)),
            pltpu.SemaphoreType.DMA((PARTS, nz)),
            pltpu.SemaphoreType.DMA((nz,)),
            pltpu.SemaphoreType.DMA((ny,)),
            pltpu.SemaphoreType.DMA((nz,)),
        ],
        compiler_params=pltpu.CompilerParams(
            collective_id=0, has_side_effects=True, vmem_limit_bytes=53 * 1024 * 1024 + 256 * 1024
        ),
        name="chain",
    )(
        panels.swapaxes(1, 2), listed.reshape(1, -1), trail_inverse, couplings,
        diag_terms.swapaxes(1, 2),
    )
    return panel.swapaxes(1, 2), diag.swapaxes(1, 2)


def solution(mesh):
    in_specs = (P("row", "col"), P(None, "row", "col"), P(), P(None, None, "col"), P())
    out_specs = (P(None, "row", "col"), P(None, None, "col"))
    return jax.shard_map(
        on_device, mesh=mesh, in_specs=in_specs, out_specs=out_specs, check_vma=False
    )
```

```python
import functools

import jax
import jax.numpy as jnp
from jax import lax
from jax.experimental import pallas as pl
from jax.experimental.pallas import tpu as pltpu
from jax.sharding import PartitionSpec as P

SUPER = 4
NX = 4
ROWS = 384
PIECE = 128
PARTS = 4
LAG = 2
ADD = 4
MESH = pl.DeviceIdType.MESH
F32 = jnp.float32
BF16 = jnp.bfloat16
NT_DIMS = (((1,), (1,)), ((), ()))
TN_DIMS = (((0,), (0,)), ((), ()))


def iota(shape, dim):
    return lax.broadcasted_iota(jnp.int32, shape, dim)


def mod(value, size):
    value = jnp.where(value < 0, value + size, value)
    return jnp.where(value >= size, value - size, value)


def split(value):
    high = value.astype(BF16)
    return [high, (value - high.astype(F32)).astype(BF16)]


def swap_halves(value):
    return pltpu.roll(value, 64, 1)


def kernel(
    ny,
    panels_ref, listed_ref, trail_ref, coup_ref, diag_ref,
    outp_ref, outd_ref,
    tp, cc, ct, vst, dgo, dgs, mw, ms, held, out, got, sp, rb, ss, zs, zb, zo, ps, pb, ev, eb1, eb2, fb,
    sem, zrecv, xrecv, precv, yrecv, frecv,
):
    nz = ny
    width = 64 * ny
    chain_rows = ROWS // ny
    tiles = width // 128
    row, col = lax.axis_index("row"), lax.axis_index("col")
    z, x = lax.div(row, NX), lax.rem(row, NX)
    y, h = lax.div(col, 2), lax.rem(col, 2)
    sibling = 1 - h

    def dev(xx, yy, zz, hh):
        return (zz * NX + xx, yy * 2 + hh)

    def remote(src, dst, send, recv, device):
        return pltpu.make_async_remote_copy(
            src_ref=src, dst_ref=dst, send_sem=send, recv_sem=recv,
            device_id=device, device_id_type=MESH,
        )

    def wait_bytes(ref, semaphore):
        pltpu.make_async_copy(ref, ref, semaphore).wait()

    (s_t, s_z, s_x, s_mw, s_p2, s_eb, s_td, r_td, s_tp, r_tp, s_rs, r_rs, s_ss, r_ss, s_zb, r_zb,
     s_mf, r_mf, s_zo, r_zo, s_p, r_p, s_e, r_e1, r_e2, s_f, r_f, s_dg, r_dg,
     l_tp, l_cc, l_dg) = [sem.at[i] for i in range(32)]

    barrier = pltpu.get_barrier_semaphore()

    def greet(device):
        pl.semaphore_signal(barrier, inc=1, device_id=device, device_id_type=MESH)

    greet(dev(x, y, z, sibling))
    for step in (1, nz - 1) if nz > 2 else (1,):
        greet(dev(x, y, mod(z + step, nz), h))
    for step in (1, NX - 1):
        greet(dev(mod(x + step, NX), y, z, h))
    for step in range(1, ny):
        greet(dev(x, mod(y + step, ny), z, h))

    @pl.when(y != z)
    def _():
        greet(dev(x, z, y, h))

    pair = x + 1 - 2 * lax.rem(x, 2)
    inner = jnp.where(jnp.logical_or(x == 1, x == 2), 1, 0)

    def side_of(core):
        return jnp.where(core == inner, 0, 1)

    kept_side, given_side = side_of(h), 1 - side_of(h)
    own_tp = pltpu.make_async_copy(
        trail_ref.at[:, pl.ds(pl.multiple_of(kept_side * ROWS, ROWS), ROWS)], tp.at[h, 0], l_tp
    )
    own_tp.start()
    own_cc = pltpu.make_async_copy(coup_ref, cc, l_cc)
    own_cc.start()
    diag_tile = diag_ref.at[x, :, pl.ds(pl.multiple_of(lax.div(z, 2) * 128, 128), 128)]
    own_dg = pltpu.make_async_copy(diag_tile, dgo, l_dg)
    own_dg.start()

    listed = listed_ref[...]

    def flag(block):
        return jnp.max(jnp.where(listed == block, 1.0, 0.0), axis=1, keepdims=True)

    lane = iota((1, ROWS), 1)
    piece_mask = jnp.where(
        lane < 128, flag(3 * row), jnp.where(lane < 256, flag(3 * row + 1), flag(3 * row + 2))
    )
    for k in range(SUPER):
        turned = panels_ref[k].astype(F32)
        mw[h, y, 32 * k:32 * (k + 1), :] = (turned * piece_mask).astype(BF16)

    pl.semaphore_wait(
        barrier, min(2, nz - 1) + NX - 1 + ny - 1 + jnp.where(y != z, 1, 0)
    )

    mine = mw.at[h, y]
    size = PIECE // PARTS
    parts = [pl.ds(size * part, size) for part in range(PARTS)]

    for part in range(PARTS):
        target = ms.at[y * NX + x, parts[part]]

        @pl.when(y != z)
        def _():
            remote(mine.at[parts[part]], target, s_t, zrecv.at[part, 0], dev(x, z, y, h)).start()

        @pl.when(y == z)
        def _():
            pltpu.make_async_copy(mine.at[parts[part]], target, zrecv.at[part, 0]).start()

    given = trail_ref.at[:, pl.ds(pl.multiple_of(given_side * ROWS, ROWS), ROWS)]
    remote(given, tp.at[h, 1], s_tp, r_tp, dev(pair, y, z, h)).start()
    send_dg = remote(diag_tile, dgs, s_dg, r_dg, dev(x, y, z, sibling))
    send_dg.start()

    def near(step):
        half = lax.div(step + 1, 2)
        return jnp.where(lax.rem(step, 2) == 1, half, mod(-half, nz))

    home = ms.at[z * NX + x]

    def relay_piece(step, part):
        slot = ms.at[mod(z - near(step), nz) * NX + x, parts[part]]
        z_next = mod(z + jnp.where(lax.rem(step, 2) == 1, 1, -1), nz)
        wait_bytes(slot, zrecv.at[part, step])

        @pl.when(step == 0)
        def _():
            remote(slot, slot, s_z, zrecv.at[part, 1], dev(x, y, mod(z + 1, nz), h)).start()

        @pl.when(step < nz - 2)
        def _():
            remote(slot, slot, s_z, zrecv.at[part, step + 2], dev(x, y, z_next, h)).start()

        remote(slot, slot, s_x, xrecv.at[part, step], dev(3 - x, y, z, h)).start()

    def relay_wide(step):
        wide = mw.at[h, mod(y - near(step), ny)]
        y_next = mod(y + jnp.where(lax.rem(step, 2) == 1, 1, -1), ny)

        @pl.when(step > 0)
        def _():
            wait_bytes(wide, yrecv.at[step])

        @pl.when(step == 0)
        def _():
            remote(wide, wide, s_mw, yrecv.at[1], dev(x, mod(y + 1, ny), z, h)).start()

        @pl.when(step < ny - 2)
        def _():
            remote(wide, wide, s_mw, yrecv.at[step + 2], dev(x, y_next, z, h)).start()

    @pl.loop(0, nz + ADD)
    def _(step):
        @pl.when(step < nz)
        def _():
            for part in range(PARTS):
                relay_piece(step, part)

        @pl.when(step < nz)
        def _():
            relay_wide(step)

        @pl.when(step == LAG - 2)
        def _():
            own_tp.wait()
            wait_bytes(tp.at[0, 0], r_tp)
            remote(tp.at[h], tp.at[h], s_td, r_td, dev(x, y, z, sibling)).start()

        @pl.when(step == LAG)
        def _():
            wait_bytes(tp.at[0], r_td)

        @pl.when(jnp.logical_and(step >= LAG, step < nz + LAG))
        def _():
            at = step - LAG
            chunk = mod(z - near(at), nz)
            for part in range(PARTS):
                wait_bytes(home.at[parts[part]], xrecv.at[part, at])
            sums = [None, None]
            for core in range(2):
                piece = ms[chunk * NX + 2 * core + side_of(core)]
                for rows in range(2):
                    term = lax.dot_general(
                        tp[core, rows], piece, NT_DIMS, preferred_element_type=F32
                    )
                    sums[rows] = term if core == 0 else sums[rows] + term
            held[chunk] = sums[0]
            out[chunk] = sums[1].astype(BF16)
            remote(out.at[chunk], got.at[chunk], s_p2, precv.at[at], dev(pair, y, z, h)).start()

        @pl.when(step >= ADD)
        def _():
            at = step - ADD
            chunk = mod(z - near(at), nz)
            wait_bytes(got.at[chunk], precv.at[at])
            total = held[chunk] + got[chunk].astype(F32)
            total = total.astype(BF16)
            lanes = pl.ds(pl.multiple_of(chunk * PIECE, PIECE), PIECE)
            for yy in range(ny):
                sp[yy, :, lanes] = total[chain_rows * yy:chain_rows * (yy + 1)]

            for i in range(1, ny):
                to = mod(y + i, ny)
                remote(
                    sp.at[to, :, lanes], rb.at[i - 1, :, lanes], s_rs, r_rs, dev(x, to, z, h)
                ).start()

    send_mf = remote(mw.at[h], mw.at[h], s_mf, r_mf, dev(x, y, z, sibling))
    send_mf.start()

    own_cc.wait()
    wide_eye = jnp.where(iota((width, width), 0) == iota((width, width), 1), 1.0, 0.0)
    wide_eye = wide_eye.astype(BF16)
    group = lax.div(iota((width, 128), 1), 32)
    picks = iota((width, 128), 0) == col * 32 + lax.rem(iota((width, 128), 1), 32)
    for j in range(SUPER - 1):
        ct[j] = lax.dot_general(
            wide_eye, cc[j], NT_DIMS, preferred_element_type=F32
        ).astype(BF16)
    above = None
    for j in reversed(range(SUPER)):
        chosen = jnp.where(jnp.logical_and(picks, group == j), 1.0, 0.0)
        if above is not None:
            chosen = chosen + jnp.dot(cc[j], above, preferred_element_type=F32)
        above = chosen.astype(BF16)
        vst[j] = above

    own_dg.wait()
    wait_bytes(dgs, r_dg)
    both = jnp.concatenate([dgo[...], dgs[...], jnp.zeros((64, 128), F32)], axis=0)
    both = jnp.where(lax.rem(z, 2) == 0, both, swap_halves(both)).T
    diag_packed = jnp.where(iota((32, 128), 1) < 64, both[0:32], swap_halves(both[32:64]))

    wait_bytes(rb, r_rs)
    for t in range(ny):
        lanes = slice(128 * t, 128 * (t + 1))
        total = sp[y, :, lanes].astype(F32)
        for i in range(ny - 1):
            total = total + rb[i, :, lanes].astype(F32)
        ss[h, :, lanes] = total
    send_ss = remote(ss.at[h], ss.at[h], s_ss, r_ss, dev(x, y, z, sibling))
    send_ss.start()
    wait_bytes(ss.at[0], r_ss)

    block = lax.shift_right_logical(
        ROWS * row + chain_rows * y + iota((chain_rows, 1), 0), 7
    )
    row_mask = jnp.max(jnp.where(listed == block, 1.0, 0.0), axis=1, keepdims=True)
    quarter = lax.div(iota((chain_rows, 128), 1), 32)
    low = iota((chain_rows, 128), 1) < 64
    result = None
    kept = []
    for k in range(SUPER):
        found = []
        for t in range(tiles):
            tile = None
            for g in range(4):
                yy = 2 * t + g // 2
                source = ss[g % 2, :, 128 * yy:128 * (yy + 1)]
                shift = (32 * (g - k)) % 128
                if shift:
                    source = pltpu.roll(source, shift, 1)
                tile = source if tile is None else jnp.where(quarter == g, source, tile)
            found.append(tile)
        summed = jnp.concatenate(found, axis=1) if tiles > 1 else found[0]
        carried = jnp.zeros_like(summed)
        if k > 0:
            carried = jnp.dot(result, cc[k - 1], preferred_element_type=F32)
            summed = summed + carried
        result = (-(summed * row_mask)).astype(BF16)
        kept.append(jnp.where(h == 0, result.astype(F32), carried))
    for two in range(SUPER // 2):
        for t in range(tiles):
            tile = slice(128 * t, 128 * (t + 1))
            first, second = kept[2 * two][:, tile], kept[2 * two + 1][:, tile]
            lanes = slice(128 * two, 128 * (two + 1))
            zs[2 * t, :, lanes] = jnp.where(low, first, swap_halves(second)).astype(BF16)
            zs[2 * t + 1, :, lanes] = jnp.where(low, swap_halves(first), second).astype(BF16)

    own_rows = pl.ds(pl.multiple_of(chain_rows * y, 16), chain_rows)

    for i in range(1, ny):
        to = mod(y + i, ny)
        remote(zs.at[to], zb.at[own_rows], s_zb, r_zb, dev(x, to, z, h)).start()

    zb[own_rows, :] = zs[y]
    wait_bytes(mw.at[0], r_mf)
    wait_bytes(zb.at[pl.ds(0, chain_rows * (ny - 1))], r_zb)

    @pl.when(h == 0)
    def _():
        remote(zb, zo, s_zo, r_zo, dev(x, y, z, 1)).start()

    low32 = iota((32, 128), 1) < 64
    for k in range(SUPER):
        left = jnp.concatenate(
            [mw[c % 2, c // 2, 32 * k:32 * (k + 1), :] for c in range(2 * ny)], axis=0
        )
        two = k // 2
        product = jnp.dot(
            left, zb[:, 128 * two:128 * (two + 1)], preferred_element_type=F32
        )
        for zz in range(nz):
            upper = product[64 * zz:64 * zz + 32]
            lower = product[64 * zz + 32:64 * zz + 64]
            if k % 2 == 0:
                packed = jnp.where(low32, upper, swap_halves(lower))
            else:
                packed = jnp.where(low32, swap_halves(upper), lower)
            ps[k * nz + zz] = packed.astype(BF16)

    far_first = sorted(
        range(1, NX * nz),
        key=lambda i: (-min(i % nz, nz - i % nz), -min(i // nz, NX - i // nz), i),
    )
    for i in far_first:
        xx, zz = mod(x + i // nz, NX), mod(z + i % nz, nz)
        remote(ps.at[xx * nz + zz], pb.at[i - 1], s_p, r_p, dev(xx, y, zz, h)).start()

    own_lane = 64 * lax.div(iota((128, 256), 0), 32) + 32 * h + lax.rem(iota((128, 256), 0), 32)
    own_lane = jnp.where(iota((128, 256), 1) == own_lane, 1.0, 0.0).astype(BF16)

    def write_panel(source):
        turned = lax.dot_general(own_lane, source[...], NT_DIMS, preferred_element_type=F32)
        outp_ref[...] = turned.astype(BF16).reshape(SUPER, 32, ROWS)

    @pl.when(h == 0)
    def _():
        write_panel(zb)

    @pl.when(h == 1)
    def _():
        wait_bytes(zo, r_zo)
        write_panel(zo)

    wait_bytes(pb, r_p)
    total = ps[x * nz + z].astype(F32)
    for i in range(NX * nz - 1):
        total = total + pb[i].astype(F32)
    ev[...] = jnp.where(h == 0, diag_packed - total, total)

    @pl.when(h == 0)
    def _():
        for i in range(1, ny):
            remote(ev, eb1.at[y], s_e, r_e1, dev(x, mod(y + i, ny), z, 0)).start()
        eb1[y] = ev[...]
        wait_bytes(eb1.at[pl.ds(0, ny - 1)], r_e1)
        remote(eb1, eb1, s_eb, r_e2, dev(x, y, z, 1)).start()

    @pl.when(h == 1)
    def _():
        for i in range(1, ny):
            remote(ev, eb2.at[z], s_e, r_e1, dev(x, mod(y + i, ny), y, 1)).start()

        @pl.when(y == z)
        def _():
            pltpu.make_async_copy(ev, eb2.at[z], r_e1).start()

        @pl.when(y != z)
        def _():
            remote(ev, eb2.at[z], s_e, r_e1, dev(x, y, y, 1)).start()

        wait_bytes(eb2, r_e1)
        remote(eb2, eb2, s_eb, r_e2, dev(x, y, z, 0)).start()

    wait_bytes(eb1, r_e2)
    upper, lower = [], []
    for t in range(tiles):
        first, second = eb1[2 * t], eb1[2 * t + 1]
        upper.append(jnp.where(low32, first, swap_halves(second)))
        lower.append(jnp.where(low32, swap_halves(first), second))
    if tiles > 1:
        upper = jnp.concatenate(upper, axis=1)
        lower = jnp.concatenate(lower, axis=1)
    else:
        upper, lower = upper[0], lower[0]
    straight = jnp.concatenate(split(jnp.concatenate([upper, lower], axis=0)), axis=0)
    stack = []
    for b in range(nz):
        stack += [eb2[b], swap_halves(eb2[b])]
    high, rest = split(jnp.concatenate(stack, axis=0))
    stack = jnp.where(
        iota((width, 128), 1) < 64, high.astype(F32), swap_halves(rest.astype(F32))
    ).astype(BF16)
    right_side = vst[x]
    own = jnp.dot(straight, right_side, preferred_element_type=F32)
    own = own + lax.dot_general(stack, right_side, TN_DIMS, preferred_element_type=F32)
    own = own[0:64] + own[64:128]
    mine_f = fb.at[x * nz + z]
    mine_f[...] = own.astype(BF16)
    order = [(i + 1) // 2 if i % 2 else nz - i // 2 for i in range(1, nz)]
    for delta in order:
        remote(mine_f, mine_f, s_f, frecv.at[delta], dev(x, y, mod(z + delta, nz), h)).start()
    for delta in [0] + order:
        slot = fb.at[x * nz + mod(z - delta, nz)]
        if delta:
            wait_bytes(slot, frecv.at[delta])
        for i in (2, 1, 3):
            remote(slot, slot, s_f, r_f, dev(mod(x + i, NX), y, z, h)).start()
    wait_bytes(fb.at[pl.ds(0, (NX - 1) * nz)], r_f)
    state = fb[pl.ds(0, nz)].reshape(width, 128).astype(F32)
    for j in range(SUPER - 1):
        moved = jnp.dot(
            ct[j], jnp.concatenate(split(state), axis=1), preferred_element_type=F32
        )
        moved = moved[:, 0:128] + moved[:, 128:256]
        added = fb[pl.ds((j + 1) * nz, nz)].reshape(width, 128).astype(F32)
        state = added + jnp.where(group > j, moved, state)
    outd_ref[...] = state.T.reshape(SUPER, 32, width)

    @pl.when(y != z)
    def _():
        wait_bytes(home, s_t)

    wait_bytes(tp.at[0, 0], s_tp)
    wait_bytes(tp.at[0], s_td)
    wait_bytes(dgs, s_dg)
    wait_bytes(ms.at[pl.ds(0, nz - 1)], s_z)
    wait_bytes(mw.at[0, pl.ds(0, ny - 1)], s_mw)
    wait_bytes(ms.at[pl.ds(0, nz)], s_x)
    wait_bytes(got, s_p2)
    wait_bytes(rb, s_rs)
    wait_bytes(mw.at[0], s_mf)
    wait_bytes(ss.at[0], s_ss)
    wait_bytes(zb.at[pl.ds(0, chain_rows * (ny - 1))], s_zb)

    @pl.when(h == 0)
    def _():
        wait_bytes(zo, s_zo)

    wait_bytes(pb, s_p)
    wait_bytes(eb1.at[pl.ds(0, ny - 1)], s_e)
    wait_bytes(eb1, s_eb)

    @pl.when(jnp.logical_and(h == 1, y != z))
    def _():
        wait_bytes(ev, s_e)

    wait_bytes(fb.at[pl.ds(0, nz - 1)], s_f)
    wait_bytes(fb.at[pl.ds(0, (NX - 1) * nz)], s_f)


def on_device(trail_inverse, panels, couplings, diag_terms, listed):
    ny = lax.axis_size("col") // 2
    nz = ny
    width = 64 * ny
    chain_rows = ROWS // ny
    vmem = pl.BlockSpec(memory_space=pltpu.VMEM)
    anywhere = pl.BlockSpec(memory_space=pltpu.HBM)
    panel, diag = pl.pallas_call(
        functools.partial(kernel, ny),
        out_shape=(
            jax.ShapeDtypeStruct((SUPER, 32, ROWS), BF16),
            jax.ShapeDtypeStruct((SUPER, 32, width), F32),
        ),
        in_specs=[vmem, vmem, anywhere, anywhere, anywhere],
        out_specs=(vmem, vmem),
        scratch_shapes=[
            pltpu.VMEM((2, 2, ROWS, ROWS), BF16),
            pltpu.VMEM((SUPER - 1, width, width), BF16),
            pltpu.VMEM((SUPER - 1, width, width), BF16),
            pltpu.VMEM((SUPER, width, 128), BF16),
            pltpu.VMEM((32, 128), F32),
            pltpu.VMEM((32, 128), F32),
            pltpu.VMEM((2, ny, PIECE, ROWS), BF16),
            pltpu.VMEM((nz * NX, PIECE, ROWS), BF16),
            pltpu.VMEM((nz, ROWS, PIECE), F32),
            pltpu.VMEM((nz, ROWS, PIECE), BF16),
            pltpu.VMEM((nz, ROWS, PIECE), BF16),
            pltpu.VMEM((ny, chain_rows, 128 * ny), BF16),
            pltpu.VMEM((ny - 1, chain_rows, 128 * ny), BF16),
            pltpu.VMEM((2, chain_rows, 128 * ny), F32),
            pltpu.VMEM((ny, chain_rows, 256), BF16),
            pltpu.VMEM((ROWS, 256), BF16),
            pltpu.VMEM((ROWS, 256), BF16),
            pltpu.VMEM((NX * nz, 32, 128), BF16),
            pltpu.VMEM((NX * nz - 1, 32, 128), BF16),
            pltpu.VMEM((32, 128), F32),
            pltpu.VMEM((ny, 32, 128), F32),
            pltpu.VMEM((nz, 32, 128), F32),
            pltpu.VMEM((NX * nz, 64, 128), BF16),
            pltpu.SemaphoreType.DMA((32,)),
            pltpu.SemaphoreType.DMA((PARTS, nz)),
            pltpu.SemaphoreType.DMA((PARTS, nz)),
            pltpu.SemaphoreType.DMA((nz,)),
            pltpu.SemaphoreType.DMA((ny,)),
            pltpu.SemaphoreType.DMA((nz,)),
        ],
        compiler_params=pltpu.CompilerParams(
            collective_id=0, has_side_effects=True, vmem_limit_bytes=53 * 1024 * 1024 + 256 * 1024
        ),
        name="chain",
    )(
        panels.swapaxes(1, 2), listed.reshape(1, -1), trail_inverse, couplings,
        diag_terms.swapaxes(1, 2),
    )
    return panel.swapaxes(1, 2), diag.swapaxes(1, 2)


def solution(mesh):
    in_specs = (P("row", "col"), P(None, "row", "col"), P(), P(None, None, "col"), P())
    out_specs = (P(None, "row", "col"), P(None, None, "col"))
    return jax.shard_map(
        on_device, mesh=mesh, in_specs=in_specs, out_specs=out_specs, check_vma=False
    )
```
